256 devices in a mesh: gx: 16 (over x, y_hi, core), gy: 16 (over y_lo, z).
Axes of the slice: x: 4, y: 4 (y_hi: 2, y_lo: 2; y = y_hi * 2 + y_lo), z: 8, core: 2. Of those that a mesh axis runs over, the one named last changes fastest.
Arguments:
- stencil: float32 [3, 3, 3, 64, 512, 512], P(None, None, None, 'gx', 'gy'), may hold values from -1 to 30, as said below
Outputs:
- level_one: float32 [3, 3, 3, 32, 256, 512], P(None, None, None, 'gx', 'gy')
- level_two: float32 [3, 3, 3, 16, 128, 512], P(None, None, None, 'gx', 'gy')
The draws below stay inside these ranges and needn't reach their ends.
Inputs may be any that keep to these rules, and one draw needn't show every extreme that they name: `stencil`: the centre coefficient (offset index 1, 1, 1) of every cell exceeds the sum of magnitudes of its 26 other coefficients; the others are not positive.
All inputs are finite; a program needn't handle non-finite values.
Results may differ from the reference program's by a relative error of at most 0.00002.
Values sent between devices are 32-bit elements; how exact they have to be, the bound alone decides.
A program may use at most 128 MiB of HBM per device.

```python
import math
import jax
import jax.numpy as jnp
from jax import lax

NZ = 512
NX = 64
NY = 512


def draw_stencil(key, part):
    key = jax.random.fold_in(key, 1)
    shape = (3, 3, 3, NX, NY, NZ)
    first, second = jax.random.split(key)
    magnitude = jnp.exp(jax.random.uniform(first, shape, jnp.float32, math.log(0.05), 0.0))
    centre = jax.random.uniform(second, shape, jnp.float32, 27.0, 30.0)
    is_centre = (lax.broadcasted_iota(jnp.int32, shape, 0) == 1) & (lax.broadcasted_iota(jnp.int32, shape, 1) == 1) & (lax.broadcasted_iota(jnp.int32, shape, 2) == 1)
    return jnp.where(is_centre, centre, -magnitude)


def setup_inputs(seed: int = 0) -> dict:
    seeds = jax.random.split(jax.random.key(seed), 2)
    return {
        "stencil": draw_stencil(jax.random.fold_in(seeds[1], 71), 0),
    }


def boundary_mask(coeffs, x_start, y_start, x_total, y_total):
    shape = coeffs.shape
    off_x = lax.broadcasted_iota(jnp.int32, shape, 0) - 1
    off_y = lax.broadcasted_iota(jnp.int32, shape, 1) - 1
    off_z = lax.broadcasted_iota(jnp.int32, shape, 2) - 1
    cell_x = lax.broadcasted_iota(jnp.int32, shape, 3) + x_start
    cell_y = lax.broadcasted_iota(jnp.int32, shape, 4) + y_start
    cell_z = lax.broadcasted_iota(jnp.int32, shape, 5)
    inside = (cell_x >= 0) & (cell_x < x_total) & (cell_y >= 0) & (cell_y < y_total)
    inside = inside & (cell_x + off_x >= 0) & (cell_x + off_x < x_total)
    inside = inside & (cell_y + off_y >= 0) & (cell_y + off_y < y_total)
    inside = inside & (cell_z + off_z >= 0) & (cell_z + off_z < shape[5])
    return jnp.where(inside, coeffs, jnp.zeros_like(coeffs))


def weight_of(shift):
    return 1.0 if shift == 0 else 0.5


def coarsen_dim(extended, odim, sdim):
    length = extended.shape[sdim]
    count = (length - 2) // 2
    fine_rows = {}
    for a in (-1, 0, 1):
        fine_rows[a] = lax.slice_in_dim(extended, a + 1, a + 2 * count, 2, sdim)
    results = []
    for o in (-1, 0, 1):
        total = None
        for s in (-1, 0, 1):
            for a in (-1, 0, 1):
                m = a + s - 2 * o
                if abs(m) <= 1:
                    term = (weight_of(a) * weight_of(m)) * lax.index_in_dim(fine_rows[a], s + 1, odim, keepdims=False)
                    total = term if total is None else total + term
        results.append(total)
    return jnp.stack(results, axis=odim)


def galerkin(coeffs):
    ext_x = jnp.pad(coeffs, ((0, 0), (0, 0), (0, 0), (1, 1), (0, 0), (0, 0)))
    part = coarsen_dim(ext_x, 0, 3)
    ext_y = jnp.pad(part, ((0, 0), (0, 0), (0, 0), (0, 0), (1, 1), (0, 0)))
    return coarsen_dim(ext_y, 1, 4)


def reference(stencil):
    x_total = stencil.shape[3]
    y_total = stencil.shape[4]
    fine = boundary_mask(stencil, 0, 0, x_total, y_total)
    level_one = boundary_mask(galerkin(fine), 0, 0, x_total // 2, y_total // 2)
    level_two = boundary_mask(galerkin(level_one), 0, 0, x_total // 4, y_total // 4)
    return level_one, level_two
```

```python
import jax
import jax.numpy as jnp
from jax import lax
from jax.experimental import pallas as pl
from jax.experimental.pallas import tpu as pltpu
from jax.sharding import PartitionSpec as P

MESH = pl.DeviceIdType.MESH
F32 = jnp.float32
TOP = 8


def odd_parts(minus, centre, plus):
    half = 0.5 * centre
    return minus + half, half + plus


def even_parts(minus, centre, plus):
    return minus, minus + (centre + centre) + plus, plus


def transfer_kernel(
    n_x, n_y, z_run, stencil, level, second, fine, p_out, p_in, q_out, q_in, y_out, y_in, d_out, d_in,
    load_sem, p_send, p_recv, q_send, q_recv, edge_send, edge_recv, ready,
):
    gx, gy = lax.axis_index("gx"), lax.axis_index("gy")
    rows, nz = stencil.shape[4], stencil.shape[5]
    half, quarter = rows // 2, rows // 4
    chunks = nz // 128
    units = 3 * chunks
    fine_unit, level_unit = TOP + rows, TOP + half
    has_next_x, has_next_y = gx < n_x - 1, gy < n_y - 1
    has_prev_x, has_prev_y = gx > 0, gy > 0
    run_start, run_end = lax.rem(gy, z_run) == 0, lax.rem(gy, z_run) == z_run - 1

    def load(x, u):
        lanes = pl.ds(pl.multiple_of(u // 3 * 128, 128), 128)
        return pltpu.make_async_copy(
            stencil.at[:, :, lax.rem(u, 3), x, :, lanes],
            fine.at[x, :, :, pl.ds(pl.multiple_of(u * fine_unit + TOP, 8), rows), :],
            load_sem.at[x, u],
        )

    def over(count, body):
        def step(i, carry):
            body(i)
            return carry

        lax.fori_loop(0, count, step, 0)

    for x in (3, 1, 2, 0):
        over(units, lambda u: load(x, u).start())

    barrier = pltpu.get_barrier_semaphore()

    def tell(condition, x, y):
        @pl.when(condition)
        def _():
            pl.semaphore_signal(barrier, inc=1, device_id=(x, y), device_id_type=MESH)

    tell(has_prev_x, gx - 1, gy)
    tell(has_next_y & ~run_end, gx, gy + 1)
    tell(has_next_y & ~run_end & has_next_x, gx + 1, gy + 1)
    tell(has_prev_y & run_start, gx, gy - 1)
    tell(has_prev_y & run_start & has_prev_x, gx - 1, gy - 1)

    def p_part(u):
        return pl.ds(pl.multiple_of(u * half, 8), half)

    def s_part(u):
        return pl.ds(pl.multiple_of(u * quarter, 8), quarter)

    def inner(u):
        return pl.ds(pl.multiple_of(u * level_unit + TOP, 8), half)

    zero_row = jnp.zeros((1, 128), F32)

    def clear_fine(u, carry):
        for ox in range(3):
            for oy in range(3):
                for x in range(4):
                    fine[x, ox, oy, pl.ds(u * fine_unit + TOP - 1, 1), :] = zero_row
                for i_x in range(2):
                    level[i_x, ox, oy, pl.ds(u * level_unit + TOP - 1, 1), :] = zero_row
        return carry

    lax.fori_loop(0, units, clear_fine, 0)

    @pl.when(~has_prev_x)
    def _():
        def clear(u, carry):
            for ox in range(2):
                for oy in range(3):
                    p_in[ox, oy, p_part(u)] = jnp.zeros((half, 128), F32)
            q_in[u] = jnp.zeros(q_in.shape[1:], F32)
            return carry

        lax.fori_loop(0, units, clear, 0)

    @pl.when(~has_prev_y)
    def _():
        y_in[...] = jnp.zeros(y_in.shape, F32)

    @pl.when(~(has_prev_x & has_prev_y))
    def _():
        d_in[...] = jnp.zeros(d_in.shape, F32)

    row16 = lax.broadcasted_iota(jnp.int32, (half, 128), 0)
    row8 = lax.broadcasted_iota(jnp.int32, (quarter, 128), 0)
    keep_first = jnp.where((row16 == 0) & ~has_prev_y, 0.0, 1.0).astype(F32)
    keep_last = jnp.where((row16 == half - 1) & ~has_next_y, 0.0, 1.0).astype(F32)
    keep_last2 = jnp.where((row8 == quarter - 1) & ~has_next_y, 0.0, 1.0).astype(F32)
    keep_x0 = jnp.where(has_prev_x, 1.0, 0.0).astype(F32)
    keep_x1 = jnp.where(has_next_x, 1.0, 0.0).astype(F32)

    def outside_z(chunk, oz, lane):
        first = (oz == 0) & (chunk == 0) & (lane == 0)
        return first | ((oz == 2) & (chunk == chunks - 1) & (lane == 127))

    def quarter_z(u):
        lane = lax.broadcasted_iota(jnp.int32, (1, 128), 1)
        return jnp.where(outside_z(u // 3, lax.rem(u, 3), lane), 0.0, 0.25).astype(F32)

    def fold(read, keep_low, keep_high):
        before, behind = odd_parts(*(read(oy, TOP - 1) for oy in range(3)))
        ahead_0, ahead_1 = odd_parts(*(read(oy, TOP + 1) for oy in range(3)))
        own = [read(oy, TOP) for oy in range(3)]
        if keep_low is not None:
            own[0] = own[0] * keep_low
        e_minus, e_zero, e_plus = even_parts(*own)
        return before + e_minus, behind + e_zero + ahead_0, (e_plus + ahead_1) * keep_high

    def fold_fine(u, ox, x):
        def read(oy, first):
            return fine[x, ox, oy, pl.ds(u * fine_unit + first, half, stride=2), :]

        return fold(read, keep_first, keep_last)

    def fold_level(u, ox, i_x):
        def read(oy, first):
            return level[i_x, ox, oy, pl.ds(u * level_unit + first, quarter, stride=2), :]

        return fold(read, None, keep_last2)

    def send_p(c):
        part = pl.ds(pl.multiple_of(c * 3 * half, 8), 3 * half)
        return pltpu.make_async_remote_copy(
            p_out.at[:, :, part], p_in.at[:, :, part], p_send.at[c], p_recv.at[c], device_id=(gx + 1, gy), device_id_type=MESH
        )

    def p_unit(u):
        load(3, u).wait()
        scale = quarter_z(u)
        f = [fold_fine(u, ox, 3) for ox in range(3)]
        for oy in range(3):
            a, b = odd_parts(f[0][oy], f[1][oy], f[2][oy])
            p_out[0, oy, p_part(u)] = a * scale
            p_out[1, oy, p_part(u)] = b * scale

    def p_step(c):
        over(3, lambda oz: p_unit(c * 3 + oz))

        @pl.when(c == 0)
        def _():
            waits = (
                has_next_x.astype(jnp.int32)
                + (has_prev_y & ~run_start).astype(jnp.int32)
                + (has_prev_y & ~run_start & has_prev_x).astype(jnp.int32)
                + (has_next_y & run_end).astype(jnp.int32)
                + (has_next_y & run_end & has_next_x).astype(jnp.int32)
            )

            @pl.when(waits > 0)
            def _():
                pl.semaphore_wait(barrier, waits)

        @pl.when(has_next_x)
        def _():
            send_p(c).start()

    over(chunks, p_step)

    @pl.when(has_prev_y & ~run_start)
    def _():
        pl.semaphore_signal(ready.at[0], inc=1, device_id=(gx, gy - 1), device_id_type=MESH)

    @pl.when(has_prev_y & ~run_start & has_prev_x)
    def _():
        pl.semaphore_signal(ready.at[1], inc=1, device_id=(gx - 1, gy - 1), device_id_type=MESH)

    def second_row(u):
        load(1, u).wait()
        load(2, u).wait()
        scale = quarter_z(u)
        f1 = [fold_fine(u, ox, 1) for ox in range(3)]
        f2 = [fold_fine(u, ox, 2) for ox in range(3)]
        for oy in range(3):
            a, b = odd_parts(f1[0][oy], f1[1][oy], f1[2][oy])
            e = even_parts(f2[0][oy], f2[1][oy], f2[2][oy])
            level[0, 1, oy, inner(u), :] = a * scale
            level[0, 2, oy, inner(u), :] = b * scale
            level[1, 0, oy, inner(u), :] = (a + e[0]) * scale
            level[1, 1, oy, inner(u), :] = (b + e[1]) * scale + p_out[0, oy, p_part(u)]
            level[1, 2, oy, inner(u), :] = (e[2] * scale + p_out[1, oy, p_part(u)]) * keep_x1

    over(units, second_row)

    def first_row(u):
        load(0, u).wait()
        scale = quarter_z(u)
        f = [fold_fine(u, ox, 0) for ox in range(3)]
        for oy in range(3):
            e = even_parts(f[0][oy] * keep_x0, f[1][oy], f[2][oy])
            level[0, 0, oy, inner(u), :] = e[0] * scale
            level[0, 1, oy, inner(u), :] += e[1] * scale
            level[0, 2, oy, inner(u), :] += e[2] * scale

    over(units, first_row)

    def fine_edge(x, ox, oy):
        return fine[x, ox, oy, pl.ds(fine_unit - 1, units, stride=fine_unit), :]

    def level_at(row):
        return pl.ds(TOP + row, units, stride=level_unit)

    def p_edge(ox, oy):
        return p_out[ox, oy, pl.ds(half - 1, units, stride=half), :]

    def group(i):
        return pl.ds(i * units, units)

    unit = lax.broadcasted_iota(jnp.int32, (units, 128), 0)
    lane = lax.broadcasted_iota(jnp.int32, (units, 128), 1)
    scale = jnp.where(outside_z(unit // 3, lax.rem(unit, 3), lane), 0.0, 0.25).astype(F32)
    h = [[odd_parts(*(fine_edge(x, ox, oy) for oy in range(3))) for ox in range(3)] for x in range(4)]
    ahead = []
    for oy in range(2):
        a3, b3 = odd_parts(*(h[3][ox][oy] for ox in range(3)))
        a1, b1 = odd_parts(*(h[1][ox][oy] for ox in range(3)))
        e2 = even_parts(*(h[2][ox][oy] for ox in range(3)))
        e0 = even_parts(h[0][0][oy] * keep_x0, h[0][1][oy], h[0][2][oy])
        d_out[group(oy), :] = a3 * scale
        d_out[group(2 + oy), :] = b3 * scale
        y_out[group(oy), :] = e0[0] * scale
        y_out[group(2 + oy), :] = (e0[1] + a1) * scale
        y_out[group(4 + oy), :] = (e0[2] + b1) * scale
        ahead.append([(a1 + e2[0]) * scale, (b1 + e2[1] + a3) * scale, (e2[2] + b3) * scale * keep_x1])
        for ox in range(3):
            y_out[group(6 + ox * 2 + oy), :] = ahead[oy][ox]
    g = [
        [odd_parts(*(level[i_x, ox, oy, level_at(half - 1), :] for oy in range(3))) for ox in range(3)]
        for i_x in range(2)
    ]
    behind = [odd_parts(*(p_edge(ox, oy) for oy in range(3))) for ox in range(2)]
    onto = [odd_parts(*(ahead[oy][ox] for ox in range(3))) for oy in range(2)]
    for oy in range(2):
        a, b = odd_parts(*(g[1][ox][oy] for ox in range(3)))
        e = even_parts(*(g[0][ox][oy] for ox in range(3)))
        y_out[group(12 + oy), :] = e[0] * 0.25
        y_out[group(14 + oy), :] = (e[1] + a) * 0.25
        y_out[group(16 + oy), :] = (e[2] + b) * (0.25 * keep_x1)
        p_minus = behind[0][oy]
        p_zero = behind[0][oy] + (behind[1][oy] + behind[1][oy])
        onto_y = [onto[0][k] if oy == 0 else onto[0][k] + (onto[1][k] + onto[1][k]) for k in range(2)]
        d_out[group(4 + oy), :] = (a + p_minus + onto_y[0]) * 0.25
        d_out[group(6 + oy), :] = (b + p_zero + onto_y[1]) * 0.25

    send_y = pltpu.make_async_remote_copy(
        y_out, y_in, edge_send.at[0], edge_recv.at[0], device_id=(gx, gy + 1), device_id_type=MESH
    )
    send_d = pltpu.make_async_remote_copy(
        d_out, d_in, edge_send.at[1], edge_recv.at[1], device_id=(gx + 1, gy + 1), device_id_type=MESH
    )

    @pl.when(has_next_y)
    def _():
        @pl.when(~run_end)
        def _():
            pl.semaphore_wait(ready.at[0], 1)

        send_y.start()

    @pl.when(has_next_x & has_next_y)
    def _():
        @pl.when(~run_end)
        def _():
            pl.semaphore_wait(ready.at[1], 1)

        send_d.start()

    def send_q(c):
        part = pl.ds(c * 3, 3)
        return pltpu.make_async_remote_copy(
            q_out.at[part], q_in.at[part], q_send.at[c], q_recv.at[c], device_id=(gx + 1, gy), device_id_type=MESH
        )

    def q_unit(u):
        f = [fold_level(u, ox, 1) for ox in range(3)]
        for oy in range(3):
            a, b = odd_parts(f[0][oy], f[1][oy], f[2][oy])
            q_out[u, 0, oy] = a * 0.25
            q_out[u, 1, oy] = b * 0.25

    def q_step(c):
        over(3, lambda oz: q_unit(c * 3 + oz))

        @pl.when(has_next_x)
        def _():
            send_q(c).start()

    over(chunks, q_step)

    @pl.when(has_prev_y)
    def _():
        send_y.wait_recv()

    @pl.when(has_prev_x & has_prev_y)
    def _():
        send_d.wait_recv()

    for i_x in range(2):
        for ox in range(3):
            for oy in range(2):
                value = y_in[group(i_x * 6 + ox * 2 + oy), :]
                if i_x == 0 and ox < 2:
                    value = value + d_in[group(ox * 2 + oy), :]
                level[i_x, ox, oy, level_at(0), :] = level[i_x, ox, oy, level_at(0), :] + value

    def finish_one(u):
        for oy in range(3):
            for ox in range(2):
                level[0, ox, oy, inner(u), :] += p_in[ox, oy, p_part(u)]
        f0 = [fold_level(u, ox, 0) for ox in range(3)]
        f1 = [fold_level(u, ox, 1) for ox in range(3)]
        for oy in range(3):
            e = even_parts(f0[0][oy], f0[1][oy], f0[2][oy])
            a, b = odd_parts(f1[0][oy], f1[1][oy], f1[2][oy])
            second[0, oy, s_part(u)] = e[0] * 0.25
            second[1, oy, s_part(u)] = (e[1] + a) * 0.25
            second[2, oy, s_part(u)] = (e[2] + b) * (0.25 * keep_x1)

    def finish_one_step(c):
        @pl.when(has_prev_x)
        def _():
            send_p(c).wait_recv()

        over(3, lambda oz: finish_one(c * 3 + oz))

    over(chunks, finish_one_step)

    for ox in range(3):
        for oy in range(2):
            value = y_in[group(12 + ox * 2 + oy), :]
            if ox < 2:
                value = value + d_in[group(4 + ox * 2 + oy), :]
            at = pl.ds(0, units, stride=quarter)
            second[ox, oy, at, :] = second[ox, oy, at, :] + value

    def finish_two_step(c):
        @pl.when(has_prev_x)
        def _():
            send_q(c).wait_recv()

        for oz in range(3):
            for ox in range(2):
                for oy in range(3):
                    second[ox, oy, s_part(c * 3 + oz)] += q_in[c * 3 + oz, ox, oy]

    over(chunks, finish_two_step)

    @pl.when(has_next_x)
    def _():
        for c in range(chunks):
            send_p(c).wait_send()
            send_q(c).wait_send()

    @pl.when(has_next_y)
    def _():
        send_y.wait_send()

    @pl.when(has_next_x & has_next_y)
    def _():
        send_d.wait_send()


def write_kernel(level, second, one, two, sem):
    half, quarter, chunks = one.shape[4], two.shape[4], one.shape[5] // 128
    copies = []
    for u in range(3 * chunks):
        oz, lanes = u % 3, pl.ds(u // 3 * 128, 128)
        for i_x in range(2):
            source = level.at[i_x, :, :, pl.ds(u * (TOP + half) + TOP, half), :]
            copies.append(pltpu.make_async_copy(source, one.at[:, :, oz, i_x, :, lanes], sem.at[u, i_x]))
        source = second.at[:, :, pl.ds(u * quarter, quarter), :]
        copies.append(pltpu.make_async_copy(source, two.at[:, :, oz, 0, :, lanes], sem.at[u, 2]))
    for copy in copies:
        copy.start()
    for copy in copies:
        copy.wait()


def solution(mesh):
    n_x, n_y = mesh.shape["gx"], mesh.shape["gy"]
    z_run = n_y // 2

    def shard(stencil):
        _, _, _, cells_x, rows, nz = stencil.shape
        half, quarter, chunks = rows // 2, rows // 4, nz // 128
        units = 3 * chunks
        vmem, hbm = pl.BlockSpec(memory_space=pltpu.VMEM), pl.BlockSpec(memory_space=pl.ANY)

        def kernel(*refs):
            transfer_kernel(n_x, n_y, z_run, *refs)

        level, second = pl.pallas_call(
            kernel,
            out_shape=(
                pltpu.VMEM((2, 3, 3, units * (TOP + half), 128), F32),
                pltpu.VMEM((3, 3, units * quarter, 128), F32),
            ),
            in_specs=[hbm],
            out_specs=(vmem, vmem),
            scratch_shapes=[
                pltpu.VMEM((cells_x, 3, 3, units * (TOP + rows), 128), F32),
                pltpu.VMEM((2, 3, units * half, 128), F32),
                pltpu.VMEM((2, 3, units * half, 128), F32),
                pltpu.VMEM((units, 2, 3, quarter, 128), F32),
                pltpu.VMEM((units, 2, 3, quarter, 128), F32),
                pltpu.VMEM((18 * units, 128), F32),
                pltpu.VMEM((18 * units, 128), F32),
                pltpu.VMEM((8 * units, 128), F32),
                pltpu.VMEM((8 * units, 128), F32),
                pltpu.SemaphoreType.DMA((cells_x, units)),
                pltpu.SemaphoreType.DMA((chunks,)),
                pltpu.SemaphoreType.DMA((chunks,)),
                pltpu.SemaphoreType.DMA((chunks,)),
                pltpu.SemaphoreType.DMA((chunks,)),
                pltpu.SemaphoreType.DMA((2,)),
                pltpu.SemaphoreType.DMA((2,)),
                pltpu.SemaphoreType.REGULAR((2,)),
            ],
            compiler_params=pltpu.CompilerParams(
                collective_id=0, has_side_effects=True, vmem_limit_bytes=56 * 2**20
            ),
        )(stencil)
        return pl.pallas_call(
            write_kernel,
            out_shape=(
                jax.ShapeDtypeStruct((3, 3, 3, cells_x // 2, half, nz), F32),
                jax.ShapeDtypeStruct((3, 3, 3, cells_x // 4, quarter, nz), F32),
            ),
            in_specs=[vmem, vmem],
            out_specs=(hbm, hbm),
            scratch_shapes=[pltpu.SemaphoreType.DMA((units, 3))],
        )(level, second)

    spec = P(None, None, None, "gx", "gy", None)
    return jax.shard_map(shard, mesh=mesh, in_specs=(spec,), out_specs=(spec, spec), check_vma=False)
```

```python
import jax
import jax.numpy as jnp
from jax import lax
from jax.experimental import pallas as pl
from jax.experimental.pallas import tpu as pltpu
from jax.sharding import PartitionSpec as P

MESH = pl.DeviceIdType.MESH
F32 = jnp.float32
TOP = 8


def odd_parts(minus, centre, plus):
    half = 0.5 * centre
    return minus + half, half + plus


def even_parts(minus, centre, plus):
    return minus, minus + (centre + centre) + plus, plus


def transfer_kernel(
    n_x, n_y, z_run, stencil, level, second, fine, p_out, p_in, q_out, q_in, y_out, y_in, d_out, d_in,
    load_sem, edge_sem, p_send, p_recv, q_send, q_recv, edge_send, edge_recv, ready,
):
    gx, gy = lax.axis_index("gx"), lax.axis_index("gy")
    rows, nz = stencil.shape[4], stencil.shape[5]
    half, quarter = rows // 2, rows // 4
    chunks = nz // 128
    fine_unit, level_unit = TOP + rows, TOP + half
    has_next_x, has_next_y = gx < n_x - 1, gy < n_y - 1
    has_prev_x, has_prev_y = gx > 0, gy > 0
    run_start, run_end = lax.rem(gy, z_run) == 0, lax.rem(gy, z_run) == z_run - 1

    def load(x, c, first, count, sem):
        lanes = pl.ds(pl.multiple_of(c * 128, 128), 128)
        return pltpu.make_async_copy(
            stencil.at[:, :, :, x, pl.ds(first, count), lanes],
            fine.at[x, :, :, :, pl.ds(pl.multiple_of(c * fine_unit + TOP + first, 8), count), :],
            sem,
        )

    def load_last_x(c):
        return load(3, c, 0, rows, load_sem.at[3, c])

    def load_body(x, c):
        return load(x, c, 0, rows - 8, load_sem.at[x, c])

    def load_edge(x, c):
        return load(x, c, rows - 8, 8, edge_sem.at[x, c])

    def over(count, body):
        def step(i, carry):
            body(i)
            return carry

        lax.fori_loop(0, count, step, 0)

    over(chunks, lambda c: load_last_x(c).start())

    barrier = pltpu.get_barrier_semaphore()

    def tell(condition, x, y):
        @pl.when(condition)
        def _():
            pl.semaphore_signal(barrier, inc=1, device_id=(x, y), device_id_type=MESH)

    tell(has_prev_x, gx - 1, gy)
    tell(has_next_y & ~run_end, gx, gy + 1)
    tell(has_next_y & ~run_end & has_next_x, gx + 1, gy + 1)
    tell(has_prev_y & run_start, gx, gy - 1)
    tell(has_prev_y & run_start & has_prev_x, gx - 1, gy - 1)

    def inner(c):
        return pl.ds(pl.multiple_of(c * level_unit + TOP, 8), half)

    def s_part(c):
        return pl.ds(pl.multiple_of(c * quarter, 8), quarter)

    zero_row = jnp.zeros((1, 128), F32)

    def clear_fine(x):
        def clear(c):
            for ox in range(3):
                for oy in range(3):
                    for oz in range(3):
                        fine[x, ox, oy, oz, pl.ds(c * fine_unit + TOP - 1, 1), :] = zero_row

        over(chunks, clear)

    def clear_level(c):
        for ox in range(3):
            for oy in range(3):
                for oz in range(3):
                    for i_x in range(2):
                        level[i_x, ox, oy, oz, pl.ds(c * level_unit + TOP - 1, 1), :] = zero_row

    clear_fine(3)

    @pl.when(~has_prev_x)
    def _():
        def clear(c):
            p_in[c] = jnp.zeros(p_in.shape[1:], F32)
            q_in[c] = jnp.zeros(q_in.shape[1:], F32)

        over(chunks, clear)

    @pl.when(~has_prev_y)
    def _():
        y_in[...] = jnp.zeros(y_in.shape, F32)

    @pl.when(~(has_prev_x & has_prev_y))
    def _():
        d_in[...] = jnp.zeros(d_in.shape, F32)

    row16 = lax.broadcasted_iota(jnp.int32, (half, 128), 0)
    row8 = lax.broadcasted_iota(jnp.int32, (quarter, 128), 0)
    keep_first = jnp.where((row16 == 0) & ~has_prev_y, 0.0, 1.0).astype(F32)
    keep_last = jnp.where((row16 == half - 1) & ~has_next_y, 0.0, 1.0).astype(F32)
    keep_last2 = jnp.where((row8 == quarter - 1) & ~has_next_y, 0.0, 1.0).astype(F32)
    keep_x0 = jnp.where(has_prev_x, 1.0, 0.0).astype(F32)
    keep_x1 = jnp.where(has_next_x, 1.0, 0.0).astype(F32)

    def quarter_z(c, oz, row_is_chunk=False):
        lane = lax.broadcasted_iota(jnp.int32, (chunks if row_is_chunk else 1, 128), 1)
        if row_is_chunk:
            c = lax.broadcasted_iota(jnp.int32, (chunks, 128), 0)
        outside = ((oz == 0) & (c == 0) & (lane == 0)) | ((oz == 2) & (c == chunks - 1) & (lane == 127))
        return jnp.where(outside, 0.0, 0.25).astype(F32)

    def fold(read, keep_low, keep_high):
        before, behind = odd_parts(*(read(oy, TOP - 1) for oy in range(3)))
        ahead_0, ahead_1 = odd_parts(*(read(oy, TOP + 1) for oy in range(3)))
        own = [read(oy, TOP) for oy in range(3)]
        if keep_low is not None:
            own[0] = own[0] * keep_low
        e_minus, e_zero, e_plus = even_parts(*own)
        return before + e_minus, behind + e_zero + ahead_0, (e_plus + ahead_1) * keep_high

    def fold_fine(c, oz, ox, x):
        def read(oy, first):
            return fine[x, ox, oy, oz, pl.ds(c * fine_unit + first, half, stride=2), :]

        return fold(read, keep_first, keep_last)

    def fold_level(c, oz, ox, i_x):
        def read(oy, first):
            return level[i_x, ox, oy, oz, pl.ds(c * level_unit + first, quarter, stride=2), :]

        return fold(read, None, keep_last2)

    def over_z(body):
        def step(oz, carry):
            body(oz)
            return carry

        lax.fori_loop(0, 3, step, 0)

    def send_p(c):
        return pltpu.make_async_remote_copy(
            p_out.at[c], p_in.at[c], p_send.at[c], p_recv.at[c], device_id=(gx + 1, gy), device_id_type=MESH
        )

    def p_step(c):
        load_last_x(c).wait()

        def unit(oz):
            scale = quarter_z(c, oz)
            f = [fold_fine(c, oz, ox, 3) for ox in range(3)]
            for oy in range(3):
                a, b = odd_parts(f[0][oy], f[1][oy], f[2][oy])
                p_out[c, 0, oy, oz] = a * scale
                p_out[c, 1, oy, oz] = b * scale

        over_z(unit)

        @pl.when(c == 0)
        def _():
            waits = (
                has_next_x.astype(jnp.int32)
                + (has_prev_y & ~run_start).astype(jnp.int32)
                + (has_prev_y & ~run_start & has_prev_x).astype(jnp.int32)
                + (has_next_y & run_end).astype(jnp.int32)
                + (has_next_y & run_end & has_next_x).astype(jnp.int32)
            )

            @pl.when(waits > 0)
            def _():
                pl.semaphore_wait(barrier, waits)

        @pl.when(has_next_x)
        def _():
            send_p(c).start()

        @pl.when(c == 0)
        def _():
            for x in range(3):
                over(chunks, lambda c: load_edge(x, c).start())

    over(chunks, p_step)

    for x in (1, 2, 0):
        over(chunks, lambda c: load_body(x, c).start())

    @pl.when(has_prev_y & ~run_start)
    def _():
        pl.semaphore_signal(ready.at[0], inc=1, device_id=(gx, gy - 1), device_id_type=MESH)

    @pl.when(has_prev_y & ~run_start & has_prev_x)
    def _():
        pl.semaphore_signal(ready.at[1], inc=1, device_id=(gx - 1, gy - 1), device_id_type=MESH)

    for x in range(3):
        clear_fine(x)
    over(chunks, clear_level)

    def group(i, oz):
        return pl.ds((i * 3 + oz) * chunks, chunks)

    def fold_last(oz, ox, x):
        def read(oy, back):
            return fine[x, ox, oy, oz, pl.ds(fine_unit - back, chunks, stride=fine_unit), :]

        before, behind = odd_parts(*(read(oy, 3) for oy in range(3)))
        ahead = odd_parts(*(read(oy, 1) for oy in range(3)))
        e = even_parts(*(read(oy, 2) for oy in range(3)))
        return (before + e[0], behind + e[1] + ahead[0], e[2] + ahead[1]), ahead

    def edges(oz):
        scale = quarter_z(None, oz, True)
        f = [[fold_last(oz, ox, x) for ox in range(3)] for x in range(4)]

        def across(parts):
            a3, b3 = odd_parts(*parts[3])
            a1, b1 = odd_parts(*parts[1])
            e2 = even_parts(*parts[2])
            e0 = even_parts(parts[0][0] * keep_x0, parts[0][1], parts[0][2])
            first = [e0[0] * scale, (e0[1] + a1) * scale, (e0[2] + b1) * scale]
            second_x = [(a1 + e2[0]) * scale, (b1 + e2[1] + a3) * scale, (e2[2] + b3) * scale * keep_x1]
            return first, second_x, [a3 * scale, b3 * scale]

        onto = []
        for oy in range(2):
            first, second_x, beyond = across([[f[x][ox][1][oy] for ox in range(3)] for x in range(4)])
            onto.append(odd_parts(*second_x))
            for ox in range(3):
                y_out[group(ox * 2 + oy, oz), :] = first[ox]
                y_out[group(6 + ox * 2 + oy, oz), :] = second_x[ox]
            for ox in range(2):
                d_out[group(ox * 2 + oy, oz), :] = beyond[ox]
        own = [across([[f[x][ox][0][oy] for ox in range(3)] for x in range(4)]) for oy in range(3)]
        g = [[odd_parts(*(own[oy][i][ox] for oy in range(3))) for ox in range(3 if i < 2 else 2)] for i in range(3)]
        for oy in range(2):
            a, b = odd_parts(*(g[1][ox][oy] for ox in range(3)))
            e = even_parts(*(g[0][ox][oy] for ox in range(3)))
            y_out[group(12 + oy, oz), :] = e[0] * 0.25
            y_out[group(14 + oy, oz), :] = (e[1] + a) * 0.25
            y_out[group(16 + oy, oz), :] = (e[2] + b) * (0.25 * keep_x1)
            p_minus = g[2][0][oy]
            p_zero = g[2][0][oy] + (g[2][1][oy] + g[2][1][oy])
            onto_y = [onto[0][k] if oy == 0 else onto[0][k] + (onto[1][k] + onto[1][k]) for k in range(2)]
            d_out[group(4 + oy, oz), :] = (a + p_minus + onto_y[0]) * 0.25
            d_out[group(6 + oy, oz), :] = (b + p_zero + onto_y[1]) * 0.25

    for x in range(3):
        over(chunks, lambda c: load_edge(x, c).wait())
    over_z(edges)

    send_y = pltpu.make_async_remote_copy(
        y_out, y_in, edge_send.at[0], edge_recv.at[0], device_id=(gx, gy + 1), device_id_type=MESH
    )
    send_d = pltpu.make_async_remote_copy(
        d_out, d_in, edge_send.at[1], edge_recv.at[1], device_id=(gx + 1, gy + 1), device_id_type=MESH
    )

    def send_edges(condition):
        @pl.when(condition & has_next_y)
        def _():
            @pl.when(~run_end)
            def _():
                pl.semaphore_wait(ready.at[0], 1)

            send_y.start()

        @pl.when(condition & has_next_x & has_next_y)
        def _():
            @pl.when(~run_end)
            def _():
                pl.semaphore_wait(ready.at[1], 1)

            send_d.start()

    send_edges(~run_start)

    def second_row(c):
        load_body(1, c).wait()
        load_body(2, c).wait()

        def unit(oz):
            scale = quarter_z(c, oz)
            f1 = [fold_fine(c, oz, ox, 1) for ox in range(3)]
            f2 = [fold_fine(c, oz, ox, 2) for ox in range(3)]
            for oy in range(3):
                a, b = odd_parts(f1[0][oy], f1[1][oy], f1[2][oy])
                e = even_parts(f2[0][oy], f2[1][oy], f2[2][oy])
                level[0, 1, oy, oz, inner(c), :] = a * scale
                level[0, 2, oy, oz, inner(c), :] = b * scale
                level[1, 0, oy, oz, inner(c), :] = (a + e[0]) * scale
                level[1, 1, oy, oz, inner(c), :] = (b + e[1]) * scale + p_out[c, 0, oy, oz]
                level[1, 2, oy, oz, inner(c), :] = (e[2] * scale + p_out[c, 1, oy, oz]) * keep_x1

        over_z(unit)

    over(chunks, second_row)

    def send_q(c):
        return pltpu.make_async_remote_copy(
            q_out.at[c], q_in.at[c], q_send.at[c], q_recv.at[c], device_id=(gx + 1, gy), device_id_type=MESH
        )

    def q_step(c):
        def unit(oz):
            f = [fold_level(c, oz, ox, 1) for ox in range(3)]
            for oy in range(3):
                a, b = odd_parts(f[0][oy], f[1][oy], f[2][oy])
                q_out[c, 0, oy, oz] = a * 0.25
                q_out[c, 1, oy, oz] = b * 0.25

        over_z(unit)

        @pl.when(has_next_x)
        def _():
            send_q(c).start()

    over(chunks, q_step)

    def first_row(c):
        load_body(0, c).wait()

        def unit(oz):
            scale = quarter_z(c, oz)
            f = [fold_fine(c, oz, ox, 0) for ox in range(3)]
            for oy in range(3):
                e = even_parts(f[0][oy] * keep_x0, f[1][oy], f[2][oy])
                level[0, 0, oy, oz, inner(c), :] = e[0] * scale
                level[0, 1, oy, oz, inner(c), :] += e[1] * scale
                level[0, 2, oy, oz, inner(c), :] += e[2] * scale

        over_z(unit)

    over(chunks, first_row)

    send_edges(run_start)

    @pl.when(has_prev_y)
    def _():
        send_y.wait_recv()

    @pl.when(has_prev_x & has_prev_y)
    def _():
        send_d.wait_recv()

    def add_edges(oz):
        at = pl.ds(TOP, chunks, stride=level_unit)
        for i_x in range(2):
            for ox in range(3):
                for oy in range(2):
                    value = y_in[group(i_x * 6 + ox * 2 + oy, oz), :]
                    if i_x == 0 and ox < 2:
                        value = value + d_in[group(ox * 2 + oy, oz), :]
                    level[i_x, ox, oy, oz, at, :] = level[i_x, ox, oy, oz, at, :] + value

    over_z(add_edges)

    def finish_one(c):
        @pl.when(has_prev_x)
        def _():
            send_p(c).wait_recv()

        def unit(oz):
            for oy in range(3):
                for ox in range(2):
                    level[0, ox, oy, oz, inner(c), :] += p_in[c, ox, oy, oz]
            f0 = [fold_level(c, oz, ox, 0) for ox in range(3)]
            f1 = [fold_level(c, oz, ox, 1) for ox in range(3)]
            for oy in range(3):
                e = even_parts(f0[0][oy], f0[1][oy], f0[2][oy])
                a, b = odd_parts(f1[0][oy], f1[1][oy], f1[2][oy])
                second[0, oy, oz, s_part(c), :] = e[0] * 0.25
                second[1, oy, oz, s_part(c), :] = (e[1] + a) * 0.25
                second[2, oy, oz, s_part(c), :] = (e[2] + b) * (0.25 * keep_x1)

        over_z(unit)

    over(chunks, finish_one)

    def add_edges_two(oz):
        at = pl.ds(0, chunks, stride=quarter)
        for ox in range(3):
            for oy in range(2):
                value = y_in[group(12 + ox * 2 + oy, oz), :]
                if ox < 2:
                    value = value + d_in[group(4 + ox * 2 + oy, oz), :]
                second[ox, oy, oz, at, :] = second[ox, oy, oz, at, :] + value

    over_z(add_edges_two)

    def finish_two(c):
        @pl.when(has_prev_x)
        def _():
            send_q(c).wait_recv()

        for oz in range(3):
            for ox in range(2):
                for oy in range(3):
                    second[ox, oy, oz, s_part(c), :] += q_in[c, ox, oy, oz]

    over(chunks, finish_two)

    @pl.when(has_next_x)
    def _():
        for c in range(chunks):
            send_p(c).wait_send()
            send_q(c).wait_send()

    @pl.when(has_next_y)
    def _():
        send_y.wait_send()

    @pl.when(has_next_x & has_next_y)
    def _():
        send_d.wait_send()


def write_kernel(level, second, one, two, sem):
    half, quarter, chunks = one.shape[4], two.shape[4], one.shape[5] // 128
    copies = []
    for c in range(chunks):
        lanes = pl.ds(c * 128, 128)
        for i_x in range(2):
            source = level.at[i_x, :, :, :, pl.ds(c * (TOP + half) + TOP, half), :]
            copies.append(pltpu.make_async_copy(source, one.at[:, :, :, i_x, :, lanes], sem.at[c, i_x]))
        source = second.at[:, :, :, pl.ds(c * quarter, quarter), :]
        copies.append(pltpu.make_async_copy(source, two.at[:, :, :, 0, :, lanes], sem.at[c, 2]))
    for copy in copies:
        copy.start()
    for copy in copies:
        copy.wait()


def solution(mesh):
    n_x, n_y = mesh.shape["gx"], mesh.shape["gy"]
    z_run = n_y // 2

    def shard(stencil):
        _, _, _, cells_x, rows, nz = stencil.shape
        half, quarter, chunks = rows // 2, rows // 4, nz // 128
        vmem, hbm = pl.BlockSpec(memory_space=pltpu.VMEM), pl.BlockSpec(memory_space=pl.ANY)

        def kernel(*refs):
            transfer_kernel(n_x, n_y, z_run, *refs)

        level, second = pl.pallas_call(
            kernel,
            out_shape=(
                pltpu.VMEM((2, 3, 3, 3, chunks * (TOP + half), 128), F32),
                pltpu.VMEM((3, 3, 3, chunks * quarter, 128), F32),
            ),
            in_specs=[hbm],
            out_specs=(vmem, vmem),
            scratch_shapes=[
                pltpu.VMEM((cells_x, 3, 3, 3, chunks * (TOP + rows), 128), F32),
                pltpu.VMEM((chunks, 2, 3, 3, half, 128), F32),
                pltpu.VMEM((chunks, 2, 3, 3, half, 128), F32),
                pltpu.VMEM((chunks, 2, 3, 3, quarter, 128), F32),
                pltpu.VMEM((chunks, 2, 3, 3, quarter, 128), F32),
                pltpu.VMEM((54 * chunks, 128), F32),
                pltpu.VMEM((54 * chunks, 128), F32),
                pltpu.VMEM((24 * chunks, 128), F32),
                pltpu.VMEM((24 * chunks, 128), F32),
                pltpu.SemaphoreType.DMA((cells_x, chunks)),
                pltpu.SemaphoreType.DMA((cells_x - 1, chunks)),
                pltpu.SemaphoreType.DMA((chunks,)),
                pltpu.SemaphoreType.DMA((chunks,)),
                pltpu.SemaphoreType.DMA((chunks,)),
                pltpu.SemaphoreType.DMA((chunks,)),
                pltpu.SemaphoreType.DMA((2,)),
                pltpu.SemaphoreType.DMA((2,)),
                pltpu.SemaphoreType.REGULAR((2,)),
            ],
            compiler_params=pltpu.CompilerParams(
                collective_id=0, has_side_effects=True, vmem_limit_bytes=56 * 2**20
            ),
        )(stencil)
        level, second = (pltpu.with_memory_space_constraint(v, pltpu.VMEM) for v in (level, second))
        return pl.pallas_call(
            write_kernel,
            out_shape=(
                jax.ShapeDtypeStruct((3, 3, 3, cells_x // 2, half, nz), F32),
                jax.ShapeDtypeStruct((3, 3, 3, cells_x // 4, quarter, nz), F32),
            ),
            in_specs=[vmem, vmem],
            out_specs=(hbm, hbm),
            scratch_shapes=[pltpu.SemaphoreType.DMA((chunks, 3))],
            compiler_params=pltpu.CompilerParams(vmem_limit_bytes=2**20),
        )(level, second)

    spec = P(None, None, None, "gx", "gy", None)
    return jax.shard_map(shard, mesh=mesh, in_specs=(spec,), out_specs=(spec, spec), check_vma=False)
```

```python
import jax
import jax.numpy as jnp
from jax import lax
from jax.experimental import pallas as pl
from jax.experimental.pallas import tpu as pltpu
from jax.sharding import PartitionSpec as P

MESH = pl.DeviceIdType.MESH
F32 = jnp.float32
TOP = 8


def odd_parts(minus, centre, plus):
    half = 0.5 * centre
    return minus + half, half + plus


def even_parts(minus, centre, plus):
    return minus, minus + (centre + centre) + plus, plus


def transfer_kernel(
    n_x, n_y, z_run, stencil, level, second, fine, p_out, p_in, q_out, q_in, y_out, y_in, d_out, d_in, q_relay,
    load_sem, edge_sem, p_send, p_recv, q_send, q_recv, edge_send, edge_recv, relay_sem, ready,
):
    gx, gy = lax.axis_index("gx"), lax.axis_index("gy")
    rows, nz = stencil.shape[4], stencil.shape[5]
    half, quarter = rows // 2, rows // 4
    chunks = nz // 128
    fine_unit, level_unit = TOP + rows, TOP + half
    has_next_x, has_next_y = gx < n_x - 1, gy < n_y - 1
    has_prev_x, has_prev_y = gx > 0, gy > 0
    run_start, run_end = lax.rem(gy, z_run) == 0, lax.rem(gy, z_run) == z_run - 1
    first_core = lax.rem(gx, 2) == 0
    second_core = ~first_core
    giver = run_end & has_next_y
    paced = giver & second_core & has_next_x
    hand_late = giver & (gx == n_x - 2)
    low_y = lax.rem(gx, 4) < 2
    arrived_first = jnp.where(low_y, 1, 1)
    sent_first = jnp.where(low_y, 1, 3)
    detour = second_core & (gy == 0) & (lax.rem(gx, 4) == 1) & has_next_x
    relay = first_core & (gy == 1) & (lax.rem(gx, 4) == 2) & has_prev_x

    def load(x, c, first, count, sem):
        lanes = pl.ds(pl.multiple_of(c * 128, 128), 128)
        return pltpu.make_async_copy(
            stencil.at[:, :, :, x, pl.ds(first, count), lanes],
            fine.at[x, :, :, :, pl.ds(pl.multiple_of(c * fine_unit + TOP + first, 8), count), :],
            sem,
        )

    def load_last_x(c):
        return load(3, c, 0, rows, load_sem.at[3, c])

    def load_body(x, c):
        return load(x, c, 0, rows - 8, load_sem.at[x, c])

    def load_edge(x, c):
        return load(x, c, rows - 8, 8, edge_sem.at[x, c])

    def over(count, body):
        def step(i, carry):
            body(i)
            return carry

        lax.fori_loop(0, count, step, 0)

    over(chunks, lambda c: load_last_x(c).start())

    barrier = pltpu.get_barrier_semaphore()

    def tell(condition, x, y):
        @pl.when(condition)
        def _():
            pl.semaphore_signal(barrier, inc=1, device_id=(x, y), device_id_type=MESH)

    tell(has_prev_x, gx - 1, gy)
    tell(has_next_y & ~run_end, gx, gy + 1)
    tell(has_next_y & ~run_end & has_next_x & second_core, gx + 1, gy + 1)
    tell(has_prev_y & run_start, gx, gy - 1)
    tell(has_prev_y & run_start & has_prev_x & first_core, gx - 1, gy - 1)

    def inner(c):
        return pl.ds(pl.multiple_of(c * level_unit + TOP, 8), half)

    def s_part(c):
        return pl.ds(pl.multiple_of(c * quarter, 8), quarter)

    zero_row = jnp.zeros((1, 128), F32)

    def clear_fine(x):
        def clear(c):
            for ox in range(3):
                for oy in range(3):
                    for oz in range(3):
                        fine[x, ox, oy, oz, pl.ds(c * fine_unit + TOP - 1, 1), :] = zero_row

        over(chunks, clear)

    def clear_level(c):
        for ox in range(3):
            for oy in range(3):
                for oz in range(3):
                    for i_x in range(2):
                        level[i_x, ox, oy, oz, pl.ds(c * level_unit + TOP - 1, 1), :] = zero_row

    clear_fine(3)

    @pl.when(~has_prev_x)
    def _():
        def clear(c):
            p_in[c] = jnp.zeros(p_in.shape[1:], F32)
            q_in[c] = jnp.zeros(q_in.shape[1:], F32)

        over(chunks, clear)

    @pl.when(~has_prev_y)
    def _():
        y_in[...] = jnp.zeros(y_in.shape, F32)

    row16 = lax.broadcasted_iota(jnp.int32, (half, 128), 0)
    row8 = lax.broadcasted_iota(jnp.int32, (quarter, 128), 0)
    keep_first = jnp.where((row16 == 0) & ~has_prev_y, 0.0, 1.0).astype(F32)
    keep_last = jnp.where((row16 == half - 1) & ~has_next_y, 0.0, 1.0).astype(F32)
    keep_last2 = jnp.where((row8 == quarter - 1) & ~has_next_y, 0.0, 1.0).astype(F32)
    keep_x0 = jnp.where(has_prev_x, 1.0, 0.0).astype(F32)
    keep_x1 = jnp.where(has_next_x, 1.0, 0.0).astype(F32)

    def quarter_z(c, oz, row_is_chunk=False):
        lane = lax.broadcasted_iota(jnp.int32, (chunks if row_is_chunk else 1, 128), 1)
        if row_is_chunk:
            c = lax.broadcasted_iota(jnp.int32, (chunks, 128), 0)
        outside = ((oz == 0) & (c == 0) & (lane == 0)) | ((oz == 2) & (c == chunks - 1) & (lane == 127))
        return jnp.where(outside, 0.0, 0.25).astype(F32)

    def fold(read, keep_low, keep_high):
        before, behind = odd_parts(*(read(oy, TOP - 1) for oy in range(3)))
        ahead_0, ahead_1 = odd_parts(*(read(oy, TOP + 1) for oy in range(3)))
        own = [read(oy, TOP) for oy in range(3)]
        if keep_low is not None:
            own[0] = own[0] * keep_low
        e_minus, e_zero, e_plus = even_parts(*own)
        return before + e_minus, behind + e_zero + ahead_0, (e_plus + ahead_1) * keep_high

    def fold_fine(c, oz, ox, x):
        def read(oy, first):
            return fine[x, ox, oy, oz, pl.ds(c * fine_unit + first, half, stride=2), :]

        return fold(read, keep_first, keep_last)

    def fold_level(c, oz, ox, i_x):
        def read(oy, first):
            return level[i_x, ox, oy, oz, pl.ds(c * level_unit + first, quarter, stride=2), :]

        return fold(read, None, keep_last2)

    def over_z(body):
        def step(oz, carry):
            body(oz)
            return carry

        lax.fori_loop(0, 3, step, 0)

    def send_p(c):
        return pltpu.make_async_remote_copy(
            p_out.at[c], p_in.at[c], p_send.at[c], p_recv.at[c], device_id=(gx + 1, gy), device_id_type=MESH
        )

    def p_step(c):
        load_last_x(c).wait()

        def unit(oz):
            scale = quarter_z(c, oz)
            f = [fold_fine(c, oz, ox, 3) for ox in range(3)]
            for oy in range(3):
                a, b = odd_parts(f[0][oy], f[1][oy], f[2][oy])
                p_out[c, 0, oy, oz] = a * scale
                p_out[c, 1, oy, oz] = b * scale

        over_z(unit)

        @pl.when(c == 0)
        def _():
            waits = (
                has_next_x.astype(jnp.int32)
                + (has_prev_y & ~run_start).astype(jnp.int32)
                + (has_prev_y & ~run_start & has_prev_x & first_core).astype(jnp.int32)
                + (has_next_y & run_end).astype(jnp.int32)
                + (has_next_y & run_end & has_next_x & second_core).astype(jnp.int32)
            )

            @pl.when(waits > 0)
            def _():
                pl.semaphore_wait(barrier, waits)

                @pl.when(has_prev_y & ~run_start)
                def _():
                    pl.semaphore_signal(ready.at[0], inc=1, device_id=(gx, gy - 1), device_id_type=MESH)

                @pl.when(has_prev_y & ~run_start & has_prev_x & first_core)
                def _():
                    pl.semaphore_signal(ready.at[1], inc=1, device_id=(gx - 1, gy - 1), device_id_type=MESH)

        @pl.when(has_next_x)
        def _():
            send_p(c).start()

        @pl.when(c == 0)
        def _():
            for x in range(3):
                over(chunks, lambda c: load_edge(x, c).start())

    over(chunks, p_step)

    for x in (1, 2, 0):
        over(chunks, lambda c: load_body(x, c).start())

    for x in range(3):
        clear_fine(x)
    over(chunks, clear_level)

    def group(i, oz):
        return pl.ds((i * 3 + oz) * chunks, chunks)

    def fold_last(oz, ox, x):
        def read(oy, back):
            return fine[x, ox, oy, oz, pl.ds(fine_unit - back, chunks, stride=fine_unit), :]

        before, behind = odd_parts(*(read(oy, 3) for oy in range(3)))
        ahead = odd_parts(*(read(oy, 1) for oy in range(3)))
        e = even_parts(*(read(oy, 2) for oy in range(3)))
        return (before + e[0], behind + e[1] + ahead[0], e[2] + ahead[1]), ahead

    def edges(oz):
        scale = quarter_z(None, oz, True)
        f = [[fold_last(oz, ox, x) for ox in range(3)] for x in range(4)]

        def across(parts):
            a3, b3 = odd_parts(*parts[3])
            a1, b1 = odd_parts(*parts[1])
            e2 = even_parts(*parts[2])
            e0 = even_parts(parts[0][0] * keep_x0, parts[0][1], parts[0][2])
            first = [e0[0] * scale, (e0[1] + a1) * scale, (e0[2] + b1) * scale]
            second_x = [(a1 + e2[0]) * scale, (b1 + e2[1] + a3) * scale, (e2[2] + b3) * scale * keep_x1]
            return first, second_x, [a3 * scale, b3 * scale]

        onto = []
        for oy in range(2):
            first, second_x, beyond = across([[f[x][ox][1][oy] for ox in range(3)] for x in range(4)])
            onto.append(odd_parts(*second_x))
            for ox in range(3):
                y_out[group(ox * 2 + oy, oz), :] = first[ox]
                y_out[group(6 + ox * 2 + oy, oz), :] = second_x[ox]
            for ox in range(2):
                d_out[group(ox * 2 + oy, oz), :] = beyond[ox]
        own = [across([[f[x][ox][0][oy] for ox in range(3)] for x in range(4)]) for oy in range(3)]
        g = [[odd_parts(*(own[oy][i][ox] for oy in range(3))) for ox in range(3 if i < 2 else 2)] for i in range(3)]
        for oy in range(2):
            a, b = odd_parts(*(g[1][ox][oy] for ox in range(3)))
            e = even_parts(*(g[0][ox][oy] for ox in range(3)))
            y_out[group(12 + oy, oz), :] = e[0] * 0.25
            y_out[group(14 + oy, oz), :] = (e[1] + a) * 0.25
            y_out[group(16 + oy, oz), :] = (e[2] + b) * (0.25 * keep_x1)
            p_minus = g[2][0][oy]
            p_zero = g[2][0][oy] + (g[2][1][oy] + g[2][1][oy])
            onto_y = [onto[0][k] if oy == 0 else onto[0][k] + (onto[1][k] + onto[1][k]) for k in range(2)]
            d_out[group(4 + oy, oz), :] = (a + p_minus + onto_y[0]) * 0.25
            d_out[group(6 + oy, oz), :] = (b + p_zero + onto_y[1]) * 0.25

    for x in range(3):
        over(chunks, lambda c: load_edge(x, c).wait())
    over_z(edges)

    send_y = pltpu.make_async_remote_copy(
        y_out, y_in, edge_send.at[0], edge_recv.at[0], device_id=(gx, gy + 1), device_id_type=MESH
    )
    def copy_d(x, y, k):
        return pltpu.make_async_remote_copy(
            d_out, d_in, edge_send.at[k], edge_recv.at[k], device_id=(x, y), device_id_type=MESH
        )

    hand_d, send_d = copy_d(gx + 1, gy, 2), copy_d(gx + 1, gy + 1, 1)

    @pl.when(first_core & has_next_y & ~hand_late)
    def _():
        hand_d.start()

    @pl.when(second_core & run_end & has_next_x & has_next_y)
    def _():
        send_d.start()

    def add_corner(ref):
        for i in range(4):
            for k in (0, 1):
                to, at = pl.ds((i + 12 * k) * 3 * chunks, 3 * chunks), pl.ds((i + 4 * k) * 3 * chunks, 3 * chunks)
                ref[to, :] = ref[to, :] + d_in[at, :]

    def second_row(c):
        load_body(1, c).wait()
        load_body(2, c).wait()

        def unit(oz):
            scale = quarter_z(c, oz)
            f1 = [fold_fine(c, oz, ox, 1) for ox in range(3)]
            f2 = [fold_fine(c, oz, ox, 2) for ox in range(3)]
            for oy in range(3):
                a, b = odd_parts(f1[0][oy], f1[1][oy], f1[2][oy])
                e = even_parts(f2[0][oy], f2[1][oy], f2[2][oy])
                level[0, 1, oy, oz, inner(c), :] = a * scale
                level[0, 2, oy, oz, inner(c), :] = b * scale
                level[1, 0, oy, oz, inner(c), :] = (a + e[0]) * scale
                level[1, 1, oy, oz, inner(c), :] = (b + e[1]) * scale + p_out[c, 0, oy, oz]
                level[1, 2, oy, oz, inner(c), :] = (e[2] * scale + p_out[c, 1, oy, oz]) * keep_x1

        over_z(unit)

    over(chunks, second_row)

    def send_q(c):
        return pltpu.make_async_remote_copy(
            q_out.at[c], q_in.at[c], q_send.at[c], q_recv.at[c], device_id=(gx + 1, gy), device_id_type=MESH
        )

    detour_q = pltpu.make_async_remote_copy(
        q_out.at[0], q_relay, q_send.at[0], relay_sem.at[0], device_id=(gx + 1, gy + 1), device_id_type=MESH
    )
    relay_q = pltpu.make_async_remote_copy(
        q_relay, q_in.at[0], relay_sem.at[1], q_recv.at[0], device_id=(gx, gy - 1), device_id_type=MESH
    )

    def q_step(c):
        def unit(oz):
            f = [fold_level(c, oz, ox, 1) for ox in range(3)]
            for oy in range(3):
                a, b = odd_parts(f[0][oy], f[1][oy], f[2][oy])
                q_out[c, 0, oy, oz] = a * 0.25
                q_out[c, 1, oy, oz] = b * 0.25

        over_z(unit)

        @pl.when(has_next_x & ~(detour & (c == 0)))
        def _():
            send_q(c).start()

        @pl.when(detour & (c == 0))
        def _():
            pl.semaphore_wait(ready.at[1], 1)
            detour_q.start()

    over(chunks, q_step)

    def first_row(c):
        load_body(0, c).wait()

        def unit(oz):
            scale = quarter_z(c, oz)
            f = [fold_fine(c, oz, ox, 0) for ox in range(3)]
            for oy in range(3):
                e = even_parts(f[0][oy] * keep_x0, f[1][oy], f[2][oy])
                level[0, 0, oy, oz, inner(c), :] = e[0] * scale
                level[0, 1, oy, oz, inner(c), :] += e[1] * scale
                level[0, 2, oy, oz, inner(c), :] += e[2] * scale

        over_z(unit)

    over(chunks, first_row)

    for c in range(3):

        @pl.when(paced & (c < sent_first))
        def _():
            send_p(c).wait_send()

    @pl.when(second_core & has_next_y)
    def _():
        hand_d.wait_recv()
        add_corner(y_out)

    @pl.when(has_next_y & ~(giver & first_core & ~low_y))
    def _():
        @pl.when(~run_end)
        def _():
            pl.semaphore_wait(ready.at[0], 1)

        send_y.start()


    @pl.when(second_core & has_next_x & has_next_y & ~run_end)
    def _():
        @pl.when(~detour)
        def _():
            pl.semaphore_wait(ready.at[1], 1)

        send_d.start()

    @pl.when(relay)
    def _():
        detour_q.wait_recv()
        relay_q.start()

    def finish_one(c):
        @pl.when(has_prev_x)
        def _():
            send_p(c).wait_recv()

        def unit(oz):
            for oy in range(3):
                for ox in range(2):
                    level[0, ox, oy, oz, inner(c), :] += p_in[c, ox, oy, oz]
            f0 = [fold_level(c, oz, ox, 0) for ox in range(3)]
            f1 = [fold_level(c, oz, ox, 1) for ox in range(3)]
            for oy in range(3):
                e = even_parts(f0[0][oy], f0[1][oy], f0[2][oy])
                a, b = odd_parts(f1[0][oy], f1[1][oy], f1[2][oy])
                second[0, oy, oz, s_part(c), :] = e[0] * 0.25
                second[1, oy, oz, s_part(c), :] = (e[1] + a) * 0.25
                second[2, oy, oz, s_part(c), :] = (e[2] + b) * (0.25 * keep_x1)

        over_z(unit)

        @pl.when(giver & first_core & ~low_y & (c == arrived_first - 1))
        def _():
            send_y.start()

        @pl.when(hand_late & (c == arrived_first - 1))
        def _():
            hand_d.start()

    over(chunks, finish_one)

    def add_edges(oz):
        one_at, two_at = pl.ds(TOP, chunks, stride=level_unit), pl.ds(0, chunks, stride=quarter)
        e, o = [], []
        for oy in range(2):
            h = [[y_in[group(i_x * 6 + ox * 2 + oy, oz), :] for ox in range(3)] for i_x in range(2)]
            for i_x in range(2):
                for ox in range(3):
                    level[i_x, ox, oy, oz, one_at, :] = level[i_x, ox, oy, oz, one_at, :] + h[i_x][ox]
            e.append(even_parts(*h[0]))
            o.append(odd_parts(*h[1]))
        onto = [[e[oy][0], e[oy][1] + o[oy][0], (e[oy][2] + o[oy][1]) * keep_x1] for oy in range(2)]
        for ox in range(3):
            minus, centre = onto[0][ox], onto[0][ox] + (onto[1][ox] + onto[1][ox])
            for oy, value in ((0, minus), (1, centre)):
                value = value * 0.25 + y_in[group(12 + ox * 2 + oy, oz), :]
                second[ox, oy, oz, two_at, :] = second[ox, oy, oz, two_at, :] + value

    def finish_edges():
        send_y.wait_recv()

        @pl.when(first_core & has_prev_x)
        def _():
            send_d.wait_recv()
            add_corner(y_in)

        over_z(add_edges)

    taker = run_start & has_prev_y

    @pl.when(has_prev_y & ~run_start)
    def _():
        finish_edges()

    def finish_two(c):
        @pl.when(has_prev_x)
        def _():
            send_q(c).wait_recv()

        for oz in range(3):
            for ox in range(2):
                for oy in range(3):
                    second[ox, oy, oz, s_part(c), :] += q_in[c, ox, oy, oz]

    over(chunks, finish_two)

    @pl.when(taker)
    def _():
        finish_edges()

    @pl.when(has_next_x)
    def _():
        for c in range(chunks):
            send_q(c).wait_send()

    @pl.when(relay)
    def _():
        relay_q.wait_send()

    for c in range(chunks):

        @pl.when(has_next_x & ~(paced & (c < sent_first)))
        def _():
            send_p(c).wait_send()

    @pl.when(has_next_y)
    def _():
        send_y.wait_send()

    @pl.when(second_core & has_next_x & has_next_y)
    def _():
        send_d.wait_send()

    @pl.when(first_core & has_next_y)
    def _():
        hand_d.wait_send()


def write_kernel(level, second, one, two, sem):
    half, quarter, chunks = one.shape[4], two.shape[4], one.shape[5] // 128
    copies = []
    for c in range(chunks):
        lanes = pl.ds(c * 128, 128)
        for i_x in range(2):
            source = level.at[i_x, :, :, :, pl.ds(c * (TOP + half) + TOP, half), :]
            copies.append(pltpu.make_async_copy(source, one.at[:, :, :, i_x, :, lanes], sem.at[c, i_x]))
        source = second.at[:, :, :, pl.ds(c * quarter, quarter), :]
        copies.append(pltpu.make_async_copy(source, two.at[:, :, :, 0, :, lanes], sem.at[c, 2]))
    for copy in copies:
        copy.start()
    for copy in copies:
        copy.wait()


def solution(mesh):
    n_x, n_y = mesh.shape["gx"], mesh.shape["gy"]
    z_run = n_y // 2

    def shard(stencil):
        _, _, _, cells_x, rows, nz = stencil.shape
        half, quarter, chunks = rows // 2, rows // 4, nz // 128
        vmem, hbm = pl.BlockSpec(memory_space=pltpu.VMEM), pl.BlockSpec(memory_space=pl.ANY)

        def kernel(*refs):
            transfer_kernel(n_x, n_y, z_run, *refs)

        level, second = pl.pallas_call(
            kernel,
            out_shape=(
                pltpu.VMEM((2, 3, 3, 3, chunks * (TOP + half), 128), F32),
                pltpu.VMEM((3, 3, 3, chunks * quarter, 128), F32),
            ),
            in_specs=[hbm],
            out_specs=(vmem, vmem),
            scratch_shapes=[
                pltpu.VMEM((cells_x, 3, 3, 3, chunks * (TOP + rows), 128), F32),
                pltpu.VMEM((chunks, 2, 3, 3, half, 128), F32),
                pltpu.VMEM((chunks, 2, 3, 3, half, 128), F32),
                pltpu.VMEM((chunks, 2, 3, 3, quarter, 128), F32),
                pltpu.VMEM((chunks, 2, 3, 3, quarter, 128), F32),
                pltpu.VMEM((54 * chunks, 128), F32),
                pltpu.VMEM((54 * chunks, 128), F32),
                pltpu.VMEM((24 * chunks, 128), F32),
                pltpu.VMEM((24 * chunks, 128), F32),
                pltpu.VMEM((2, 3, 3, quarter, 128), F32),
                pltpu.SemaphoreType.DMA((cells_x, chunks)),
                pltpu.SemaphoreType.DMA((cells_x - 1, chunks)),
                pltpu.SemaphoreType.DMA((chunks,)),
                pltpu.SemaphoreType.DMA((chunks,)),
                pltpu.SemaphoreType.DMA((chunks,)),
                pltpu.SemaphoreType.DMA((chunks,)),
                pltpu.SemaphoreType.DMA((3,)),
                pltpu.SemaphoreType.DMA((3,)),
                pltpu.SemaphoreType.DMA((2,)),
                pltpu.SemaphoreType.REGULAR((2,)),
            ],
            compiler_params=pltpu.CompilerParams(
                collective_id=0, has_side_effects=True, vmem_limit_bytes=56 * 2**20
            ),
        )(stencil)
        level, second = (pltpu.with_memory_space_constraint(v, pltpu.VMEM) for v in (level, second))
        return pl.pallas_call(
            write_kernel,
            out_shape=(
                jax.ShapeDtypeStruct((3, 3, 3, cells_x // 2, half, nz), F32),
                jax.ShapeDtypeStruct((3, 3, 3, cells_x // 4, quarter, nz), F32),
            ),
            in_specs=[vmem, vmem],
            out_specs=(hbm, hbm),
            scratch_shapes=[pltpu.SemaphoreType.DMA((chunks, 3))],
            compiler_params=pltpu.CompilerParams(vmem_limit_bytes=2**20),
        )(level, second)

    spec = P(None, None, None, "gx", "gy", None)
    return jax.shard_map(shard, mesh=mesh, in_specs=(spec,), out_specs=(spec, spec), check_vma=False)
```

```python
import jax
import jax.numpy as jnp
from jax import lax
from jax.experimental import pallas as pl
from jax.experimental.pallas import tpu as pltpu
from jax.sharding import PartitionSpec as P

MESH = pl.DeviceIdType.MESH
F32 = jnp.float32
TOP = 8


def odd_parts(minus, centre, plus):
    half = 0.5 * centre
    return minus + half, half + plus


def even_parts(minus, centre, plus):
    return minus, minus + (centre + centre) + plus, plus


def transfer_kernel(
    n_x, n_y, z_run, stencil, level, second, fine, p_out, p_in, q_out, q_in, y_out, y_in, d_out, d_in, q_relay,
    load_sem, edge_sem, p_send, p_recv, q_send, q_recv, edge_send, edge_recv, relay_sem, ready,
):
    gx, gy = lax.axis_index("gx"), lax.axis_index("gy")
    rows, nz = stencil.shape[4], stencil.shape[5]
    half, quarter = rows // 2, rows // 4
    chunks = nz // 128
    fine_unit, level_unit = TOP + rows, TOP + half
    has_next_x, has_next_y = gx < n_x - 1, gy < n_y - 1
    has_prev_x, has_prev_y = gx > 0, gy > 0
    run_start, run_end = lax.rem(gy, z_run) == 0, lax.rem(gy, z_run) == z_run - 1
    first_core = lax.rem(gx, 2) == 0
    second_core = ~first_core
    giver = run_end & has_next_y
    paced = giver & second_core & has_next_x & (gx != 3)
    last = giver & (gx == n_x - 1)
    low_y = (lax.rem(gx, 4) < 2) | (gx < 4)
    arrived_first = jnp.where(low_y, 1, 1)
    sent_first = jnp.where((gx == 1) | ~low_y, 2, 1)
    detour = second_core & (gy == 0) & (lax.rem(gx, 4) == 1) & has_next_x
    relay = first_core & (gy == 1) & (lax.rem(gx, 4) == 2) & has_prev_x
    half_detour = second_core & (gy == 0) & (lax.rem(gx, 4) == 3) & has_next_x
    half_relay = first_core & (gy == 1) & (lax.rem(gx, 4) == 0) & has_prev_x

    def load(x, c, first, count, sem):
        lanes = pl.ds(pl.multiple_of(c * 128, 128), 128)
        return pltpu.make_async_copy(
            stencil.at[:, :, :, x, pl.ds(first, count), lanes],
            fine.at[x, :, :, :, pl.ds(pl.multiple_of(c * fine_unit + TOP + first, 8), count), :],
            sem,
        )

    def load_last_x(c):
        return load(3, c, 0, rows, load_sem.at[3, c])

    def load_body(x, c):
        return load(x, c, 0, rows - 8, load_sem.at[x, c])

    def load_edge(x, c):
        return load(x, c, rows - 8, 8, edge_sem.at[x, c])

    def over(count, body):
        def step(i, carry):
            body(i)
            return carry

        lax.fori_loop(0, count, step, 0)

    over(chunks, lambda c: load_last_x(c).start())

    barrier = pltpu.get_barrier_semaphore()

    def tell(condition, x, y):
        @pl.when(condition)
        def _():
            pl.semaphore_signal(barrier, inc=1, device_id=(x, y), device_id_type=MESH)

    tell(has_prev_x, gx - 1, gy)
    tell(has_next_y & ~run_end, gx, gy + 1)
    tell(has_next_y & ~run_end & has_next_x & second_core, gx + 1, gy + 1)
    tell(has_prev_y & run_start, gx, gy - 1)
    tell(has_prev_y & run_start & has_prev_x & first_core, gx - 1, gy - 1)

    def inner(c):
        return pl.ds(pl.multiple_of(c * level_unit + TOP, 8), half)

    def s_part(c):
        return pl.ds(pl.multiple_of(c * quarter, 8), quarter)

    zero_row = jnp.zeros((1, 128), F32)

    def clear_fine(x):
        def clear(c):
            for ox in range(3):
                for oy in range(3):
                    for oz in range(3):
                        fine[x, ox, oy, oz, pl.ds(c * fine_unit + TOP - 1, 1), :] = zero_row

        over(chunks, clear)

    def clear_level(c):
        for ox in range(3):
            for oy in range(3):
                for oz in range(3):
                    for i_x in range(2):
                        level[i_x, ox, oy, oz, pl.ds(c * level_unit + TOP - 1, 1), :] = zero_row

    clear_fine(3)

    @pl.when(~has_prev_x)
    def _():
        def clear(c):
            p_in[c] = jnp.zeros(p_in.shape[1:], F32)
            q_in[c] = jnp.zeros(q_in.shape[1:], F32)

        over(chunks, clear)

    @pl.when(~has_prev_y)
    def _():
        y_in[...] = jnp.zeros(y_in.shape, F32)

    row16 = lax.broadcasted_iota(jnp.int32, (half, 128), 0)
    row8 = lax.broadcasted_iota(jnp.int32, (quarter, 128), 0)
    keep_first = jnp.where((row16 == 0) & ~has_prev_y, 0.0, 1.0).astype(F32)
    keep_last = jnp.where((row16 == half - 1) & ~has_next_y, 0.0, 1.0).astype(F32)
    keep_last2 = jnp.where((row8 == quarter - 1) & ~has_next_y, 0.0, 1.0).astype(F32)
    keep_x0 = jnp.where(has_prev_x, 1.0, 0.0).astype(F32)
    keep_x1 = jnp.where(has_next_x, 1.0, 0.0).astype(F32)

    def quarter_z(c, oz, row_is_chunk=False):
        lane = lax.broadcasted_iota(jnp.int32, (chunks if row_is_chunk else 1, 128), 1)
        if row_is_chunk:
            c = lax.broadcasted_iota(jnp.int32, (chunks, 128), 0)
        outside = ((oz == 0) & (c == 0) & (lane == 0)) | ((oz == 2) & (c == chunks - 1) & (lane == 127))
        return jnp.where(outside, 0.0, 0.25).astype(F32)

    def fold(read, keep_low, keep_high):
        before, behind = odd_parts(*(read(oy, TOP - 1) for oy in range(3)))
        ahead_0, ahead_1 = odd_parts(*(read(oy, TOP + 1) for oy in range(3)))
        own = [read(oy, TOP) for oy in range(3)]
        if keep_low is not None:
            own[0] = own[0] * keep_low
        e_minus, e_zero, e_plus = even_parts(*own)
        return before + e_minus, behind + e_zero + ahead_0, (e_plus + ahead_1) * keep_high

    def fold_fine(c, oz, ox, x):
        def read(oy, first):
            return fine[x, ox, oy, oz, pl.ds(c * fine_unit + first, half, stride=2), :]

        return fold(read, keep_first, keep_last)

    def fold_level(c, oz, ox, i_x):
        def read(oy, first):
            return level[i_x, ox, oy, oz, pl.ds(c * level_unit + first, quarter, stride=2), :]

        return fold(read, None, keep_last2)

    def over_z(body):
        def step(oz, carry):
            body(oz)
            return carry

        lax.fori_loop(0, 3, step, 0)

    def send_p(c):
        return pltpu.make_async_remote_copy(
            p_out.at[c], p_in.at[c], p_send.at[c], p_recv.at[c], device_id=(gx + 1, gy), device_id_type=MESH
        )

    def p_step(c):
        load_last_x(c).wait()

        def unit(oz):
            scale = quarter_z(c, oz)
            f = [fold_fine(c, oz, ox, 3) for ox in range(3)]
            for oy in range(3):
                a, b = odd_parts(f[0][oy], f[1][oy], f[2][oy])
                p_out[c, 0, oy, oz] = a * scale
                p_out[c, 1, oy, oz] = b * scale

        over_z(unit)

        @pl.when(c == 0)
        def _():
            waits = (
                has_next_x.astype(jnp.int32)
                + (has_prev_y & ~run_start).astype(jnp.int32)
                + (has_prev_y & ~run_start & has_prev_x & first_core).astype(jnp.int32)
                + (has_next_y & run_end).astype(jnp.int32)
                + (has_next_y & run_end & has_next_x & second_core).astype(jnp.int32)
            )

            @pl.when(waits > 0)
            def _():
                pl.semaphore_wait(barrier, waits)

                @pl.when(has_prev_y & ~run_start)
                def _():
                    pl.semaphore_signal(ready.at[0], inc=1, device_id=(gx, gy - 1), device_id_type=MESH)

                @pl.when(has_prev_y & ~run_start & has_prev_x & first_core)
                def _():
                    pl.semaphore_signal(ready.at[1], inc=1, device_id=(gx - 1, gy - 1), device_id_type=MESH)

        @pl.when(has_next_x)
        def _():
            send_p(c).start()

        @pl.when(c == 0)
        def _():
            for x in range(3):
                over(chunks, lambda c: load_edge(x, c).start())

    over(chunks, p_step)

    for x in (1, 2, 0):
        over(chunks, lambda c: load_body(x, c).start())

    for x in range(3):
        clear_fine(x)
    over(chunks, clear_level)

    def group(i, oz):
        return pl.ds((i * 3 + oz) * chunks, chunks)

    def fold_last(oz, ox, x):
        def read(oy, back):
            return fine[x, ox, oy, oz, pl.ds(fine_unit - back, chunks, stride=fine_unit), :]

        before, behind = odd_parts(*(read(oy, 3) for oy in range(3)))
        ahead = odd_parts(*(read(oy, 1) for oy in range(3)))
        e = even_parts(*(read(oy, 2) for oy in range(3)))
        return (before + e[0], behind + e[1] + ahead[0], e[2] + ahead[1]), ahead

    def edges(oz):
        scale = quarter_z(None, oz, True)
        f = [[fold_last(oz, ox, x) for ox in range(3)] for x in range(4)]

        def across(parts):
            a3, b3 = odd_parts(*parts[3])
            a1, b1 = odd_parts(*parts[1])
            e2 = even_parts(*parts[2])
            e0 = even_parts(parts[0][0] * keep_x0, parts[0][1], parts[0][2])
            first = [e0[0] * scale, (e0[1] + a1) * scale, (e0[2] + b1) * scale]
            second_x = [(a1 + e2[0]) * scale, (b1 + e2[1] + a3) * scale, (e2[2] + b3) * scale * keep_x1]
            return first, second_x, [a3 * scale, b3 * scale]

        onto = []
        for oy in range(2):
            first, second_x, beyond = across([[f[x][ox][1][oy] for ox in range(3)] for x in range(4)])
            onto.append(odd_parts(*second_x))
            for ox in range(3):
                y_out[group(ox * 2 + oy, oz), :] = first[ox]
                y_out[group(6 + ox * 2 + oy, oz), :] = second_x[ox]
            for ox in range(2):
                d_out[group(ox * 2 + oy, oz), :] = beyond[ox]
        own = [across([[f[x][ox][0][oy] for ox in range(3)] for x in range(4)]) for oy in range(3)]
        g = [[odd_parts(*(own[oy][i][ox] for oy in range(3))) for ox in range(3 if i < 2 else 2)] for i in range(3)]
        for oy in range(2):
            a, b = odd_parts(*(g[1][ox][oy] for ox in range(3)))
            e = even_parts(*(g[0][ox][oy] for ox in range(3)))
            y_out[group(12 + oy, oz), :] = e[0] * 0.25
            y_out[group(14 + oy, oz), :] = (e[1] + a) * 0.25
            y_out[group(16 + oy, oz), :] = (e[2] + b) * (0.25 * keep_x1)
            p_minus = g[2][0][oy]
            p_zero = g[2][0][oy] + (g[2][1][oy] + g[2][1][oy])
            onto_y = [onto[0][k] if oy == 0 else onto[0][k] + (onto[1][k] + onto[1][k]) for k in range(2)]
            d_out[group(4 + oy, oz), :] = (a + p_minus + onto_y[0]) * 0.25
            d_out[group(6 + oy, oz), :] = (b + p_zero + onto_y[1]) * 0.25

    for x in range(3):
        over(chunks, lambda c: load_edge(x, c).wait())
    over_z(edges)

    send_y = pltpu.make_async_remote_copy(
        y_out, y_in, edge_send.at[0], edge_recv.at[0], device_id=(gx, gy + 1), device_id_type=MESH
    )
    def copy_d(x, y, k):
        return pltpu.make_async_remote_copy(
            d_out, d_in, edge_send.at[k], edge_recv.at[k], device_id=(x, y), device_id_type=MESH
        )

    hand_d, send_d = copy_d(gx + 1, gy, 2), copy_d(gx + 1, gy + 1, 1)

    @pl.when(first_core & has_next_y)
    def _():
        hand_d.start()

    @pl.when(second_core & run_end & has_next_x & has_next_y)
    def _():
        send_d.start()

    def add_corner(ref):
        for i in range(4):
            for k in (0, 1):
                to, at = pl.ds((i + 12 * k) * 3 * chunks, 3 * chunks), pl.ds((i + 4 * k) * 3 * chunks, 3 * chunks)
                ref[to, :] = ref[to, :] + d_in[at, :]

    def second_row(c):
        load_body(1, c).wait()
        load_body(2, c).wait()

        def unit(oz):
            scale = quarter_z(c, oz)
            f1 = [fold_fine(c, oz, ox, 1) for ox in range(3)]
            f2 = [fold_fine(c, oz, ox, 2) for ox in range(3)]
            for oy in range(3):
                a, b = odd_parts(f1[0][oy], f1[1][oy], f1[2][oy])
                e = even_parts(f2[0][oy], f2[1][oy], f2[2][oy])
                level[0, 1, oy, oz, inner(c), :] = a * scale
                level[0, 2, oy, oz, inner(c), :] = b * scale
                level[1, 0, oy, oz, inner(c), :] = (a + e[0]) * scale
                level[1, 1, oy, oz, inner(c), :] = (b + e[1]) * scale + p_out[c, 0, oy, oz]
                level[1, 2, oy, oz, inner(c), :] = (e[2] * scale + p_out[c, 1, oy, oz]) * keep_x1

        over_z(unit)

    over(chunks, second_row)

    def send_q(c):
        return pltpu.make_async_remote_copy(
            q_out.at[c], q_in.at[c], q_send.at[c], q_recv.at[c], device_id=(gx + 1, gy), device_id_type=MESH
        )

    detour_q = pltpu.make_async_remote_copy(
        q_out.at[0], q_relay, q_send.at[0], relay_sem.at[0], device_id=(gx + 1, gy + 1), device_id_type=MESH
    )
    relay_q = pltpu.make_async_remote_copy(
        q_relay, q_in.at[0], relay_sem.at[1], q_recv.at[0], device_id=(gx, gy - 1), device_id_type=MESH
    )

    half_detour_q = pltpu.make_async_remote_copy(
        q_out.at[0, 0], q_relay.at[0], q_send.at[0], relay_sem.at[0], device_id=(gx + 1, gy + 1), device_id_type=MESH
    )
    half_relay_q = pltpu.make_async_remote_copy(
        q_relay.at[0], q_in.at[0, 0], relay_sem.at[1], q_recv.at[0], device_id=(gx, gy - 1), device_id_type=MESH
    )
    half_direct_q = pltpu.make_async_remote_copy(
        q_out.at[0, 1], q_in.at[0, 1], q_send.at[0], q_recv.at[0], device_id=(gx + 1, gy), device_id_type=MESH
    )

    def q_step(c):
        def unit(oz):
            f = [fold_level(c, oz, ox, 1) for ox in range(3)]
            for oy in range(3):
                a, b = odd_parts(f[0][oy], f[1][oy], f[2][oy])
                q_out[c, 0, oy, oz] = a * 0.25
                q_out[c, 1, oy, oz] = b * 0.25

        over_z(unit)

        @pl.when(has_next_x & ~((detour | half_detour) & (c == 0)))
        def _():
            send_q(c).start()

        @pl.when(detour & (c == 0))
        def _():
            pl.semaphore_wait(ready.at[1], 1)
            detour_q.start()

        @pl.when(half_detour & (c == 0))
        def _():
            pl.semaphore_wait(ready.at[1], 1)
            half_detour_q.start()
            half_direct_q.start()

    over(chunks, q_step)

    def first_row(c):
        load_body(0, c).wait()

        def unit(oz):
            scale = quarter_z(c, oz)
            f = [fold_fine(c, oz, ox, 0) for ox in range(3)]
            for oy in range(3):
                e = even_parts(f[0][oy] * keep_x0, f[1][oy], f[2][oy])
                level[0, 0, oy, oz, inner(c), :] = e[0] * scale
                level[0, 1, oy, oz, inner(c), :] += e[1] * scale
                level[0, 2, oy, oz, inner(c), :] += e[2] * scale

        over_z(unit)

    over(chunks, first_row)

    for c in range(2):

        @pl.when(paced & (c < sent_first))
        def _():
            send_p(c).wait_send()

    @pl.when(second_core & has_next_y)
    def _():
        hand_d.wait_recv()
        add_corner(y_out)

    @pl.when(has_next_y & ~(giver & first_core & ~low_y) & ~last & ~(giver & (gx == 0)))
    def _():
        @pl.when(~run_end)
        def _():
            pl.semaphore_wait(ready.at[0], 1)

        send_y.start()


    @pl.when(second_core & has_next_x & has_next_y & ~run_end)
    def _():
        @pl.when(~(detour | half_detour))
        def _():
            pl.semaphore_wait(ready.at[1], 1)

        send_d.start()

    @pl.when(relay)
    def _():
        detour_q.wait_recv()
        relay_q.start()

    @pl.when(half_relay)
    def _():
        half_detour_q.wait_recv()
        half_relay_q.start()

    def finish_one(c):
        @pl.when(has_prev_x)
        def _():
            send_p(c).wait_recv()

        def unit(oz):
            for oy in range(3):
                for ox in range(2):
                    level[0, ox, oy, oz, inner(c), :] += p_in[c, ox, oy, oz]
            f0 = [fold_level(c, oz, ox, 0) for ox in range(3)]
            f1 = [fold_level(c, oz, ox, 1) for ox in range(3)]
            for oy in range(3):
                e = even_parts(f0[0][oy], f0[1][oy], f0[2][oy])
                a, b = odd_parts(f1[0][oy], f1[1][oy], f1[2][oy])
                second[0, oy, oz, s_part(c), :] = e[0] * 0.25
                second[1, oy, oz, s_part(c), :] = (e[1] + a) * 0.25
                second[2, oy, oz, s_part(c), :] = (e[2] + b) * (0.25 * keep_x1)

        over_z(unit)

        @pl.when(giver & first_core & ~low_y & (c == arrived_first - 1))
        def _():
            send_y.start()

    over(chunks, finish_one)

    @pl.when(last | (giver & (gx == 0)))
    def _():
        send_y.start()

    def add_edges(oz):
        one_at, two_at = pl.ds(TOP, chunks, stride=level_unit), pl.ds(0, chunks, stride=quarter)
        e, o = [], []
        for oy in range(2):
            h = [[y_in[group(i_x * 6 + ox * 2 + oy, oz), :] for ox in range(3)] for i_x in range(2)]
            for i_x in range(2):
                for ox in range(3):
                    level[i_x, ox, oy, oz, one_at, :] = level[i_x, ox, oy, oz, one_at, :] + h[i_x][ox]
            e.append(even_parts(*h[0]))
            o.append(odd_parts(*h[1]))
        onto = [[e[oy][0], e[oy][1] + o[oy][0], (e[oy][2] + o[oy][1]) * keep_x1] for oy in range(2)]
        for ox in range(3):
            minus, centre = onto[0][ox], onto[0][ox] + (onto[1][ox] + onto[1][ox])
            for oy, value in ((0, minus), (1, centre)):
                value = value * 0.25 + y_in[group(12 + ox * 2 + oy, oz), :]
                second[ox, oy, oz, two_at, :] = second[ox, oy, oz, two_at, :] + value

    def finish_edges():
        send_y.wait_recv()

        @pl.when(first_core & has_prev_x)
        def _():
            send_d.wait_recv()
            add_corner(y_in)

        over_z(add_edges)

    taker = run_start & has_prev_y

    @pl.when(has_prev_y & ~run_start)
    def _():
        finish_edges()

    def finish_two(c):
        @pl.when(has_prev_x)
        def _():
            send_q(c).wait_recv()

        for oz in range(3):
            for ox in range(2):
                for oy in range(3):
                    second[ox, oy, oz, s_part(c), :] += q_in[c, ox, oy, oz]

    over(chunks, finish_two)

    @pl.when(taker)
    def _():
        finish_edges()

    @pl.when(has_next_x)
    def _():
        for c in range(chunks):
            send_q(c).wait_send()

    @pl.when(relay)
    def _():
        relay_q.wait_send()

    @pl.when(half_relay)
    def _():
        half_relay_q.wait_send()

    for c in range(chunks):

        @pl.when(has_next_x & ~(paced & (c < sent_first)))
        def _():
            send_p(c).wait_send()

    @pl.when(has_next_y)
    def _():
        send_y.wait_send()

    @pl.when(second_core & has_next_x & has_next_y)
    def _():
        send_d.wait_send()

    @pl.when(first_core & has_next_y)
    def _():
        hand_d.wait_send()


def write_kernel(level, second, one, two, sem):
    half, quarter, chunks = one.shape[4], two.shape[4], one.shape[5] // 128
    copies = []
    for c in range(chunks):
        lanes = pl.ds(c * 128, 128)
        for i_x in range(2):
            source = level.at[i_x, :, :, :, pl.ds(c * (TOP + half) + TOP, half), :]
            copies.append(pltpu.make_async_copy(source, one.at[:, :, :, i_x, :, lanes], sem.at[c, i_x]))
        source = second.at[:, :, :, pl.ds(c * quarter, quarter), :]
        copies.append(pltpu.make_async_copy(source, two.at[:, :, :, 0, :, lanes], sem.at[c, 2]))
    for copy in copies:
        copy.start()
    for copy in copies:
        copy.wait()


def solution(mesh):
    n_x, n_y = mesh.shape["gx"], mesh.shape["gy"]
    z_run = n_y // 2

    def shard(stencil):
        _, _, _, cells_x, rows, nz = stencil.shape
        half, quarter, chunks = rows // 2, rows // 4, nz // 128
        vmem, hbm = pl.BlockSpec(memory_space=pltpu.VMEM), pl.BlockSpec(memory_space=pl.ANY)

        def kernel(*refs):
            transfer_kernel(n_x, n_y, z_run, *refs)

        level, second = pl.pallas_call(
            kernel,
            out_shape=(
                pltpu.VMEM((2, 3, 3, 3, chunks * (TOP + half), 128), F32),
                pltpu.VMEM((3, 3, 3, chunks * quarter, 128), F32),
            ),
            in_specs=[hbm],
            out_specs=(vmem, vmem),
            scratch_shapes=[
                pltpu.VMEM((cells_x, 3, 3, 3, chunks * (TOP + rows), 128), F32),
                pltpu.VMEM((chunks, 2, 3, 3, half, 128), F32),
                pltpu.VMEM((chunks, 2, 3, 3, half, 128), F32),
                pltpu.VMEM((chunks, 2, 3, 3, quarter, 128), F32),
                pltpu.VMEM((chunks, 2, 3, 3, quarter, 128), F32),
                pltpu.VMEM((54 * chunks, 128), F32),
                pltpu.VMEM((54 * chunks, 128), F32),
                pltpu.VMEM((24 * chunks, 128), F32),
                pltpu.VMEM((24 * chunks, 128), F32),
                pltpu.VMEM((2, 3, 3, quarter, 128), F32),
                pltpu.SemaphoreType.DMA((cells_x, chunks)),
                pltpu.SemaphoreType.DMA((cells_x - 1, chunks)),
                pltpu.SemaphoreType.DMA((chunks,)),
                pltpu.SemaphoreType.DMA((chunks,)),
                pltpu.SemaphoreType.DMA((chunks,)),
                pltpu.SemaphoreType.DMA((chunks,)),
                pltpu.SemaphoreType.DMA((3,)),
                pltpu.SemaphoreType.DMA((3,)),
                pltpu.SemaphoreType.DMA((2,)),
                pltpu.SemaphoreType.REGULAR((2,)),
            ],
            compiler_params=pltpu.CompilerParams(
                collective_id=0, has_side_effects=True, vmem_limit_bytes=56 * 2**20
            ),
        )(stencil)
        level, second = (pltpu.with_memory_space_constraint(v, pltpu.VMEM) for v in (level, second))
        return pl.pallas_call(
            write_kernel,
            out_shape=(
                jax.ShapeDtypeStruct((3, 3, 3, cells_x // 2, half, nz), F32),
                jax.ShapeDtypeStruct((3, 3, 3, cells_x // 4, quarter, nz), F32),
            ),
            in_specs=[vmem, vmem],
            out_specs=(hbm, hbm),
            scratch_shapes=[pltpu.SemaphoreType.DMA((chunks, 3))],
            compiler_params=pltpu.CompilerParams(vmem_limit_bytes=2**20),
        )(level, second)

    spec = P(None, None, None, "gx", "gy", None)
    return jax.shard_map(shard, mesh=mesh, in_specs=(spec,), out_specs=(spec, spec), check_vma=False)
```

```python
import jax
import jax.numpy as jnp
from jax import lax
from jax.experimental import pallas as pl
from jax.experimental.pallas import tpu as pltpu
from jax.sharding import PartitionSpec as P

MESH = pl.DeviceIdType.MESH
F32 = jnp.float32
TOP = 8


def odd_parts(minus, centre, plus):
    half = 0.5 * centre
    return minus + half, half + plus


def even_parts(minus, centre, plus):
    return minus, minus + (centre + centre) + plus, plus


def transfer_kernel(
    n_x, n_y, z_run, stencil, level, second, fine, p_out, p_in, q_out, q_in, y_out, y_in, d_out, d_in, q_relay,
    load_sem, edge_sem, p_send, p_recv, q_send, q_recv, edge_send, edge_recv, relay_sem, ready,
):
    gx, gy = lax.axis_index("gx"), lax.axis_index("gy")
    rows, nz = stencil.shape[4], stencil.shape[5]
    half, quarter = rows // 2, rows // 4
    chunks = nz // 128
    fine_unit, level_unit = TOP + rows, TOP + half
    has_next_x, has_next_y = gx < n_x - 1, gy < n_y - 1
    has_prev_x, has_prev_y = gx > 0, gy > 0
    run_start, run_end = lax.rem(gy, z_run) == 0, lax.rem(gy, z_run) == z_run - 1
    first_core = lax.rem(gx, 2) == 0
    second_core = ~first_core
    giver = run_end & has_next_y
    paced = giver & second_core & has_next_x & (gx != 3)
    last = giver & (gx == n_x - 1)
    low_y = (lax.rem(gx, 4) < 2) | (gx < 4)
    arrived_first = jnp.where(low_y, 1, 1)
    sent_first = jnp.where((gx == 1) | ~low_y, 2, 1)
    detour = second_core & run_start & (lax.rem(gx, 4) == 1) & has_next_x
    relay = first_core & (lax.rem(gy, z_run) == 1) & (lax.rem(gx, 4) == 2) & has_prev_x
    half_detour = second_core & run_start & (lax.rem(gx, 4) == 3) & has_next_x
    half_relay = first_core & (lax.rem(gy, z_run) == 1) & (lax.rem(gx, 4) == 0) & has_prev_x

    def load(x, c, first, count, sem):
        lanes = pl.ds(pl.multiple_of(c * 128, 128), 128)
        return pltpu.make_async_copy(
            stencil.at[:, :, :, x, pl.ds(first, count), lanes],
            fine.at[x, :, :, :, pl.ds(pl.multiple_of(c * fine_unit + TOP + first, 8), count), :],
            sem,
        )

    def load_last_x(c):
        return load(3, c, 0, rows, load_sem.at[3, c])

    def load_body(x, c):
        return load(x, c, 0, rows - 8, load_sem.at[x, c])

    def load_edge(x, c):
        return load(x, c, rows - 8, 8, edge_sem.at[x, c])

    def over(count, body):
        def step(i, carry):
            body(i)
            return carry

        lax.fori_loop(0, count, step, 0)

    over(chunks, lambda c: load_last_x(c).start())

    barrier = pltpu.get_barrier_semaphore()

    def tell(condition, x, y):
        @pl.when(condition)
        def _():
            pl.semaphore_signal(barrier, inc=1, device_id=(x, y), device_id_type=MESH)

    tell(has_prev_x, gx - 1, gy)
    tell(has_next_y & ~run_end, gx, gy + 1)
    tell(has_next_y & ~run_end & has_next_x & second_core, gx + 1, gy + 1)
    tell(has_prev_y & run_start, gx, gy - 1)
    tell(has_prev_y & run_start & has_prev_x & first_core, gx - 1, gy - 1)

    def inner(c):
        return pl.ds(pl.multiple_of(c * level_unit + TOP, 8), half)

    def s_part(c):
        return pl.ds(pl.multiple_of(c * quarter, 8), quarter)

    zero_row = jnp.zeros((1, 128), F32)

    def clear_fine(x):
        def clear(c):
            for ox in range(3):
                for oy in range(3):
                    for oz in range(3):
                        fine[x, ox, oy, oz, pl.ds(c * fine_unit + TOP - 1, 1), :] = zero_row

        over(chunks, clear)

    def clear_level(c):
        for ox in range(3):
            for oy in range(3):
                for oz in range(3):
                    for i_x in range(2):
                        level[i_x, ox, oy, oz, pl.ds(c * level_unit + TOP - 1, 1), :] = zero_row

    clear_fine(3)

    @pl.when(~has_prev_x)
    def _():
        def clear(c):
            p_in[c] = jnp.zeros(p_in.shape[1:], F32)
            q_in[c] = jnp.zeros(q_in.shape[1:], F32)

        over(chunks, clear)

    @pl.when(~has_prev_y)
    def _():
        y_in[...] = jnp.zeros(y_in.shape, F32)

    row16 = lax.broadcasted_iota(jnp.int32, (half, 128), 0)
    row8 = lax.broadcasted_iota(jnp.int32, (quarter, 128), 0)
    keep_first = jnp.where((row16 == 0) & ~has_prev_y, 0.0, 1.0).astype(F32)
    keep_last = jnp.where((row16 == half - 1) & ~has_next_y, 0.0, 1.0).astype(F32)
    keep_last2 = jnp.where((row8 == quarter - 1) & ~has_next_y, 0.0, 1.0).astype(F32)
    keep_x0 = jnp.where(has_prev_x, 1.0, 0.0).astype(F32)
    keep_x1 = jnp.where(has_next_x, 1.0, 0.0).astype(F32)

    def quarter_z(c, oz, row_is_chunk=False):
        lane = lax.broadcasted_iota(jnp.int32, (chunks if row_is_chunk else 1, 128), 1)
        if row_is_chunk:
            c = lax.broadcasted_iota(jnp.int32, (chunks, 128), 0)
        outside = ((oz == 0) & (c == 0) & (lane == 0)) | ((oz == 2) & (c == chunks - 1) & (lane == 127))
        return jnp.where(outside, 0.0, 0.25).astype(F32)

    def fold(read, keep_low, keep_high):
        before, behind = odd_parts(*(read(oy, TOP - 1) for oy in range(3)))
        ahead_0, ahead_1 = odd_parts(*(read(oy, TOP + 1) for oy in range(3)))
        own = [read(oy, TOP) for oy in range(3)]
        if keep_low is not None:
            own[0] = own[0] * keep_low
        e_minus, e_zero, e_plus = even_parts(*own)
        return before + e_minus, behind + e_zero + ahead_0, (e_plus + ahead_1) * keep_high

    def fold_fine(c, oz, ox, x):
        def read(oy, first):
            return fine[x, ox, oy, oz, pl.ds(c * fine_unit + first, half, stride=2), :]

        return fold(read, keep_first, keep_last)

    def fold_level(c, oz, ox, i_x):
        def read(oy, first):
            return level[i_x, ox, oy, oz, pl.ds(c * level_unit + first, quarter, stride=2), :]

        return fold(read, None, keep_last2)

    def over_z(body):
        def step(oz, carry):
            body(oz)
            return carry

        lax.fori_loop(0, 3, step, 0)

    def send_p(c):
        return pltpu.make_async_remote_copy(
            p_out.at[c], p_in.at[c], p_send.at[c], p_recv.at[c], device_id=(gx + 1, gy), device_id_type=MESH
        )

    def p_step(c):
        load_last_x(c).wait()

        def unit(oz):
            scale = quarter_z(c, oz)
            f = [fold_fine(c, oz, ox, 3) for ox in range(3)]
            for oy in range(3):
                a, b = odd_parts(f[0][oy], f[1][oy], f[2][oy])
                p_out[c, 0, oy, oz] = a * scale
                p_out[c, 1, oy, oz] = b * scale

        over_z(unit)

        @pl.when(c == 0)
        def _():
            waits = (
                has_next_x.astype(jnp.int32)
                + (has_prev_y & ~run_start).astype(jnp.int32)
                + (has_prev_y & ~run_start & has_prev_x & first_core).astype(jnp.int32)
                + (has_next_y & run_end).astype(jnp.int32)
                + (has_next_y & run_end & has_next_x & second_core).astype(jnp.int32)
            )

            @pl.when(waits > 0)
            def _():
                pl.semaphore_wait(barrier, waits)

                @pl.when(has_prev_y & ~run_start)
                def _():
                    pl.semaphore_signal(ready.at[0], inc=1, device_id=(gx, gy - 1), device_id_type=MESH)

                @pl.when(has_prev_y & ~run_start & has_prev_x & first_core)
                def _():
                    pl.semaphore_signal(ready.at[1], inc=1, device_id=(gx - 1, gy - 1), device_id_type=MESH)

        @pl.when(has_next_x)
        def _():
            send_p(c).start()

        @pl.when(c == 0)
        def _():
            for x in range(3):
                over(chunks, lambda c: load_edge(x, c).start())

    over(chunks, p_step)

    for x in (1, 2, 0):
        over(chunks, lambda c: load_body(x, c).start())

    for x in range(3):
        clear_fine(x)
    over(chunks, clear_level)

    def group(i, oz):
        return pl.ds((i * 3 + oz) * chunks, chunks)

    def fold_last(oz, ox, x):
        def read(oy, back):
            return fine[x, ox, oy, oz, pl.ds(fine_unit - back, chunks, stride=fine_unit), :]

        before, behind = odd_parts(*(read(oy, 3) for oy in range(3)))
        ahead = odd_parts(*(read(oy, 1) for oy in range(3)))
        e = even_parts(*(read(oy, 2) for oy in range(3)))
        return (before + e[0], behind + e[1] + ahead[0], e[2] + ahead[1]), ahead

    def edges(oz):
        scale = quarter_z(None, oz, True)
        f = [[fold_last(oz, ox, x) for ox in range(3)] for x in range(4)]

        def across(parts):
            a3, b3 = odd_parts(*parts[3])
            a1, b1 = odd_parts(*parts[1])
            e2 = even_parts(*parts[2])
            e0 = even_parts(parts[0][0] * keep_x0, parts[0][1], parts[0][2])
            first = [e0[0] * scale, (e0[1] + a1) * scale, (e0[2] + b1) * scale]
            second_x = [(a1 + e2[0]) * scale, (b1 + e2[1] + a3) * scale, (e2[2] + b3) * scale * keep_x1]
            return first, second_x, [a3 * scale, b3 * scale]

        onto = []
        for oy in range(2):
            first, second_x, beyond = across([[f[x][ox][1][oy] for ox in range(3)] for x in range(4)])
            onto.append(odd_parts(*second_x))
            for ox in range(3):
                y_out[group(ox * 2 + oy, oz), :] = first[ox]
                y_out[group(6 + ox * 2 + oy, oz), :] = second_x[ox]
            for ox in range(2):
                d_out[group(ox * 2 + oy, oz), :] = beyond[ox]
        own = [across([[f[x][ox][0][oy] for ox in range(3)] for x in range(4)]) for oy in range(3)]
        g = [[odd_parts(*(own[oy][i][ox] for oy in range(3))) for ox in range(3 if i < 2 else 2)] for i in range(3)]
        for oy in range(2):
            a, b = odd_parts(*(g[1][ox][oy] for ox in range(3)))
            e = even_parts(*(g[0][ox][oy] for ox in range(3)))
            y_out[group(12 + oy, oz), :] = e[0] * 0.25
            y_out[group(14 + oy, oz), :] = (e[1] + a) * 0.25
            y_out[group(16 + oy, oz), :] = (e[2] + b) * (0.25 * keep_x1)
            p_minus = g[2][0][oy]
            p_zero = g[2][0][oy] + (g[2][1][oy] + g[2][1][oy])
            onto_y = [onto[0][k] if oy == 0 else onto[0][k] + (onto[1][k] + onto[1][k]) for k in range(2)]
            d_out[group(4 + oy, oz), :] = (a + p_minus + onto_y[0]) * 0.25
            d_out[group(6 + oy, oz), :] = (b + p_zero + onto_y[1]) * 0.25

    for x in range(3):
        over(chunks, lambda c: load_edge(x, c).wait())
    over_z(edges)

    send_y = pltpu.make_async_remote_copy(
        y_out, y_in, edge_send.at[0], edge_recv.at[0], device_id=(gx, gy + 1), device_id_type=MESH
    )
    def copy_d(x, y, k):
        return pltpu.make_async_remote_copy(
            d_out, d_in, edge_send.at[k], edge_recv.at[k], device_id=(x, y), device_id_type=MESH
        )

    hand_d, send_d = copy_d(gx + 1, gy, 2), copy_d(gx + 1, gy + 1, 1)

    @pl.when(first_core & has_next_y)
    def _():
        hand_d.start()

    @pl.when(second_core & run_end & has_next_x & has_next_y)
    def _():
        send_d.start()

    def add_corner(ref):
        for i in range(4):
            for k in (0, 1):
                to, at = pl.ds((i + 12 * k) * 3 * chunks, 3 * chunks), pl.ds((i + 4 * k) * 3 * chunks, 3 * chunks)
                ref[to, :] = ref[to, :] + d_in[at, :]

    def second_row(c):
        load_body(1, c).wait()
        load_body(2, c).wait()

        def unit(oz):
            scale = quarter_z(c, oz)
            f1 = [fold_fine(c, oz, ox, 1) for ox in range(3)]
            f2 = [fold_fine(c, oz, ox, 2) for ox in range(3)]
            for oy in range(3):
                a, b = odd_parts(f1[0][oy], f1[1][oy], f1[2][oy])
                e = even_parts(f2[0][oy], f2[1][oy], f2[2][oy])
                level[0, 1, oy, oz, inner(c), :] = a * scale
                level[0, 2, oy, oz, inner(c), :] = b * scale
                level[1, 0, oy, oz, inner(c), :] = (a + e[0]) * scale
                level[1, 1, oy, oz, inner(c), :] = (b + e[1]) * scale + p_out[c, 0, oy, oz]
                level[1, 2, oy, oz, inner(c), :] = (e[2] * scale + p_out[c, 1, oy, oz]) * keep_x1

        over_z(unit)

    over(chunks, second_row)

    def send_q(c):
        return pltpu.make_async_remote_copy(
            q_out.at[c], q_in.at[c], q_send.at[c], q_recv.at[c], device_id=(gx + 1, gy), device_id_type=MESH
        )

    detour_q = pltpu.make_async_remote_copy(
        q_out.at[0], q_relay, q_send.at[0], relay_sem.at[0], device_id=(gx + 1, gy + 1), device_id_type=MESH
    )
    relay_q = pltpu.make_async_remote_copy(
        q_relay, q_in.at[0], relay_sem.at[1], q_recv.at[0], device_id=(gx, gy - 1), device_id_type=MESH
    )

    half_detour_q = pltpu.make_async_remote_copy(
        q_out.at[0, 0], q_relay.at[0], q_send.at[0], relay_sem.at[0], device_id=(gx + 1, gy + 1), device_id_type=MESH
    )
    half_relay_q = pltpu.make_async_remote_copy(
        q_relay.at[0], q_in.at[0, 0], relay_sem.at[1], q_recv.at[0], device_id=(gx, gy - 1), device_id_type=MESH
    )
    half_direct_q = pltpu.make_async_remote_copy(
        q_out.at[0, 1], q_in.at[0, 1], q_send.at[0], q_recv.at[0], device_id=(gx + 1, gy), device_id_type=MESH
    )

    def q_step(c):
        def unit(oz):
            f = [fold_level(c, oz, ox, 1) for ox in range(3)]
            for oy in range(3):
                a, b = odd_parts(f[0][oy], f[1][oy], f[2][oy])
                q_out[c, 0, oy, oz] = a * 0.25
                q_out[c, 1, oy, oz] = b * 0.25

        over_z(unit)

        @pl.when(has_next_x & ~((detour | half_detour) & (c == 0)))
        def _():
            send_q(c).start()

        @pl.when(detour & (c == 0))
        def _():
            pl.semaphore_wait(ready.at[1], 1)
            detour_q.start()

        @pl.when(half_detour & (c == 0))
        def _():
            pl.semaphore_wait(ready.at[1], 1)
            half_detour_q.start()
            half_direct_q.start()

    over(chunks, q_step)

    def first_row(c):
        load_body(0, c).wait()

        def unit(oz):
            scale = quarter_z(c, oz)
            f = [fold_fine(c, oz, ox, 0) for ox in range(3)]
            for oy in range(3):
                e = even_parts(f[0][oy] * keep_x0, f[1][oy], f[2][oy])
                level[0, 0, oy, oz, inner(c), :] = e[0] * scale
                level[0, 1, oy, oz, inner(c), :] += e[1] * scale
                level[0, 2, oy, oz, inner(c), :] += e[2] * scale

        over_z(unit)

    over(chunks, first_row)

    for c in range(2):

        @pl.when(paced & (c < sent_first))
        def _():
            send_p(c).wait_send()

    @pl.when(second_core & has_next_y)
    def _():
        hand_d.wait_recv()
        add_corner(y_out)

    @pl.when(has_next_y & ~(giver & first_core & ~low_y) & ~last & ~(giver & (gx == 0)))
    def _():
        @pl.when(~run_end)
        def _():
            pl.semaphore_wait(ready.at[0], 1)

        send_y.start()


    @pl.when(second_core & has_next_x & has_next_y & ~run_end)
    def _():
        @pl.when(~(detour | half_detour))
        def _():
            pl.semaphore_wait(ready.at[1], 1)

        send_d.start()

    @pl.when(relay)
    def _():
        detour_q.wait_recv()
        relay_q.start()

    @pl.when(half_relay)
    def _():
        half_detour_q.wait_recv()
        half_relay_q.start()

    def finish_one(c):
        @pl.when(has_prev_x)
        def _():
            send_p(c).wait_recv()

        def unit(oz):
            for oy in range(3):
                for ox in range(2):
                    level[0, ox, oy, oz, inner(c), :] += p_in[c, ox, oy, oz]
            f0 = [fold_level(c, oz, ox, 0) for ox in range(3)]
            f1 = [fold_level(c, oz, ox, 1) for ox in range(3)]
            for oy in range(3):
                e = even_parts(f0[0][oy], f0[1][oy], f0[2][oy])
                a, b = odd_parts(f1[0][oy], f1[1][oy], f1[2][oy])
                second[0, oy, oz, s_part(c), :] = e[0] * 0.25
                second[1, oy, oz, s_part(c), :] = (e[1] + a) * 0.25
                second[2, oy, oz, s_part(c), :] = (e[2] + b) * (0.25 * keep_x1)

        over_z(unit)

        @pl.when(giver & first_core & ~low_y & (c == arrived_first - 1))
        def _():
            send_y.start()

    over(chunks, finish_one)

    @pl.when(last | (giver & (gx == 0)))
    def _():
        send_y.start()

    def add_edges(oz):
        one_at, two_at = pl.ds(TOP, chunks, stride=level_unit), pl.ds(0, chunks, stride=quarter)
        e, o = [], []
        for oy in range(2):
            h = [[y_in[group(i_x * 6 + ox * 2 + oy, oz), :] for ox in range(3)] for i_x in range(2)]
            for i_x in range(2):
                for ox in range(3):
                    level[i_x, ox, oy, oz, one_at, :] = level[i_x, ox, oy, oz, one_at, :] + h[i_x][ox]
            e.append(even_parts(*h[0]))
            o.append(odd_parts(*h[1]))
        onto = [[e[oy][0], e[oy][1] + o[oy][0], (e[oy][2] + o[oy][1]) * keep_x1] for oy in range(2)]
        for ox in range(3):
            minus, centre = onto[0][ox], onto[0][ox] + (onto[1][ox] + onto[1][ox])
            for oy, value in ((0, minus), (1, centre)):
                value = value * 0.25 + y_in[group(12 + ox * 2 + oy, oz), :]
                second[ox, oy, oz, two_at, :] = second[ox, oy, oz, two_at, :] + value

    def finish_edges():
        send_y.wait_recv()

        @pl.when(first_core & has_prev_x)
        def _():
            send_d.wait_recv()
            add_corner(y_in)

        over_z(add_edges)

    taker = run_start & has_prev_y

    @pl.when(has_prev_y & ~run_start)
    def _():
        finish_edges()

    def finish_two(c):
        @pl.when(has_prev_x)
        def _():
            send_q(c).wait_recv()

        for oz in range(3):
            for ox in range(2):
                for oy in range(3):
                    second[ox, oy, oz, s_part(c), :] += q_in[c, ox, oy, oz]

    over(chunks, finish_two)

    @pl.when(taker)
    def _():
        finish_edges()

    @pl.when(has_next_x)
    def _():
        for c in range(chunks):
            send_q(c).wait_send()

    @pl.when(relay)
    def _():
        relay_q.wait_send()

    @pl.when(half_relay)
    def _():
        half_relay_q.wait_send()

    for c in range(chunks):

        @pl.when(has_next_x & ~(paced & (c < sent_first)))
        def _():
            send_p(c).wait_send()

    @pl.when(has_next_y)
    def _():
        send_y.wait_send()

    @pl.when(second_core & has_next_x & has_next_y)
    def _():
        send_d.wait_send()

    @pl.when(first_core & has_next_y)
    def _():
        hand_d.wait_send()


def write_kernel(level, second, one, two, sem):
    half, quarter, chunks = one.shape[4], two.shape[4], one.shape[5] // 128
    copies = []
    for c in range(chunks):
        lanes = pl.ds(c * 128, 128)
        for i_x in range(2):
            source = level.at[i_x, :, :, :, pl.ds(c * (TOP + half) + TOP, half), :]
            copies.append(pltpu.make_async_copy(source, one.at[:, :, :, i_x, :, lanes], sem.at[c, i_x]))
        source = second.at[:, :, :, pl.ds(c * quarter, quarter), :]
        copies.append(pltpu.make_async_copy(source, two.at[:, :, :, 0, :, lanes], sem.at[c, 2]))
    for copy in copies:
        copy.start()
    for copy in copies:
        copy.wait()


def solution(mesh):
    n_x, n_y = mesh.shape["gx"], mesh.shape["gy"]
    z_run = n_y // 2

    def shard(stencil):
        _, _, _, cells_x, rows, nz = stencil.shape
        half, quarter, chunks = rows // 2, rows // 4, nz // 128
        vmem, hbm = pl.BlockSpec(memory_space=pltpu.VMEM), pl.BlockSpec(memory_space=pl.ANY)

        def kernel(*refs):
            transfer_kernel(n_x, n_y, z_run, *refs)

        level, second = pl.pallas_call(
            kernel,
            out_shape=(
                pltpu.VMEM((2, 3, 3, 3, chunks * (TOP + half), 128), F32),
                pltpu.VMEM((3, 3, 3, chunks * quarter, 128), F32),
            ),
            in_specs=[hbm],
            out_specs=(vmem, vmem),
            scratch_shapes=[
                pltpu.VMEM((cells_x, 3, 3, 3, chunks * (TOP + rows), 128), F32),
                pltpu.VMEM((chunks, 2, 3, 3, half, 128), F32),
                pltpu.VMEM((chunks, 2, 3, 3, half, 128), F32),
                pltpu.VMEM((chunks, 2, 3, 3, quarter, 128), F32),
                pltpu.VMEM((chunks, 2, 3, 3, quarter, 128), F32),
                pltpu.VMEM((54 * chunks, 128), F32),
                pltpu.VMEM((54 * chunks, 128), F32),
                pltpu.VMEM((24 * chunks, 128), F32),
                pltpu.VMEM((24 * chunks, 128), F32),
                pltpu.VMEM((2, 3, 3, quarter, 128), F32),
                pltpu.SemaphoreType.DMA((cells_x, chunks)),
                pltpu.SemaphoreType.DMA((cells_x - 1, chunks)),
                pltpu.SemaphoreType.DMA((chunks,)),
                pltpu.SemaphoreType.DMA((chunks,)),
                pltpu.SemaphoreType.DMA((chunks,)),
                pltpu.SemaphoreType.DMA((chunks,)),
                pltpu.SemaphoreType.DMA((3,)),
                pltpu.SemaphoreType.DMA((3,)),
                pltpu.SemaphoreType.DMA((2,)),
                pltpu.SemaphoreType.REGULAR((2,)),
            ],
            compiler_params=pltpu.CompilerParams(
                collective_id=0, has_side_effects=True, vmem_limit_bytes=56 * 2**20
            ),
        )(stencil)
        level, second = (pltpu.with_memory_space_constraint(v, pltpu.VMEM) for v in (level, second))
        return pl.pallas_call(
            write_kernel,
            out_shape=(
                jax.ShapeDtypeStruct((3, 3, 3, cells_x // 2, half, nz), F32),
                jax.ShapeDtypeStruct((3, 3, 3, cells_x // 4, quarter, nz), F32),
            ),
            in_specs=[vmem, vmem],
            out_specs=(hbm, hbm),
            scratch_shapes=[pltpu.SemaphoreType.DMA((chunks, 3))],
            compiler_params=pltpu.CompilerParams(vmem_limit_bytes=2**20),
        )(level, second)

    spec = P(None, None, None, "gx", "gy", None)
    return jax.shard_map(shard, mesh=mesh, in_specs=(spec,), out_specs=(spec, spec), check_vma=False)
```

```python
import jax
import jax.numpy as jnp
from jax import lax
from jax.experimental import pallas as pl
from jax.experimental.pallas import tpu as pltpu
from jax.sharding import PartitionSpec as P

MESH = pl.DeviceIdType.MESH
F32 = jnp.float32
TOP = 8


def odd_parts(minus, centre, plus):
    half = 0.5 * centre
    return minus + half, half + plus


def even_parts(minus, centre, plus):
    return minus, minus + (centre + centre) + plus, plus


def transfer_kernel(
    n_x, n_y, z_run, stencil, level, second, fine, p_out, p_in, q_out, q_in, y_out, y_in, d_out, d_in, q_relay,
    load_sem, edge_sem, p_send, p_recv, q_send, q_recv, edge_send, edge_recv, relay_sem, ready,
):
    gx, gy = lax.axis_index("gx"), lax.axis_index("gy")
    rows, nz = stencil.shape[4], stencil.shape[5]
    half, quarter = rows // 2, rows // 4
    chunks = nz // 128
    fine_unit, level_unit = TOP + rows, TOP + half
    has_next_x, has_next_y = gx < n_x - 1, gy < n_y - 1
    has_prev_x, has_prev_y = gx > 0, gy > 0
    run_start, run_end = lax.rem(gy, z_run) == 0, lax.rem(gy, z_run) == z_run - 1
    first_core = lax.rem(gx, 2) == 0
    second_core = ~first_core
    giver = run_end & has_next_y
    paced = giver & second_core & has_next_x
    hand_late = giver & (gx == n_x - 2)
    low_y = lax.rem(gx, 4) < 2
    arrived_first = jnp.where(low_y, 1, 1)
    sent_first = jnp.where(low_y, 1, 3)
    detour = second_core & (gy == 0) & (lax.rem(gx, 4) == 1) & has_next_x
    relay = first_core & (gy == 1) & (lax.rem(gx, 4) == 2) & has_prev_x

    def load(x, c, first, count, sem):
        lanes = pl.ds(pl.multiple_of(c * 128, 128), 128)
        return pltpu.make_async_copy(
            stencil.at[:, :, :, x, pl.ds(first, count), lanes],
            fine.at[x, :, :, :, pl.ds(pl.multiple_of(c * fine_unit + TOP + first, 8), count), :],
            sem,
        )

    def load_last_x(c):
        return load(3, c, 0, rows, load_sem.at[3, c])

    def load_body(x, c):
        return load(x, c, 0, rows - 8, load_sem.at[x, c])

    def load_edge(x, c):
        return load(x, c, rows - 8, 8, edge_sem.at[x, c])

    def over(count, body):
        def step(i, carry):
            body(i)
            return carry

        lax.fori_loop(0, count, step, 0)

    over(chunks, lambda c: load_last_x(c).start())

    barrier = pltpu.get_barrier_semaphore()

    def tell(condition, x, y):
        @pl.when(condition)
        def _():
            pl.semaphore_signal(barrier, inc=1, device_id=(x, y), device_id_type=MESH)

    tell(has_prev_x, gx - 1, gy)
    tell(has_next_y & ~run_end, gx, gy + 1)
    tell(has_next_y & ~run_end & has_next_x & second_core, gx + 1, gy + 1)
    tell(has_prev_y & run_start, gx, gy - 1)
    tell(has_prev_y & run_start & has_prev_x & first_core, gx - 1, gy - 1)

    def inner(c):
        return pl.ds(pl.multiple_of(c * level_unit + TOP, 8), half)

    def s_part(c):
        return pl.ds(pl.multiple_of(c * quarter, 8), quarter)

    zero_row = jnp.zeros((1, 128), F32)

    def clear_fine(x):
        def clear(c):
            for ox in range(3):
                for oy in range(3):
                    for oz in range(3):
                        fine[x, ox, oy, oz, pl.ds(c * fine_unit + TOP - 1, 1), :] = zero_row

        over(chunks, clear)

    def clear_level(c):
        for ox in range(3):
            for oy in range(3):
                for oz in range(3):
                    for i_x in range(2):
                        level[i_x, ox, oy, oz, pl.ds(c * level_unit + TOP - 1, 1), :] = zero_row

    clear_fine(3)

    @pl.when(~has_prev_x)
    def _():
        def clear(c):
            p_in[c] = jnp.zeros(p_in.shape[1:], F32)
            q_in[c] = jnp.zeros(q_in.shape[1:], F32)

        over(chunks, clear)

    @pl.when(~has_prev_y)
    def _():
        y_in[...] = jnp.zeros(y_in.shape, F32)

    row16 = lax.broadcasted_iota(jnp.int32, (half, 128), 0)
    row8 = lax.broadcasted_iota(jnp.int32, (quarter, 128), 0)
    keep_first = jnp.where((row16 == 0) & ~has_prev_y, 0.0, 1.0).astype(F32)
    keep_last = jnp.where((row16 == half - 1) & ~has_next_y, 0.0, 1.0).astype(F32)
    keep_last2 = jnp.where((row8 == quarter - 1) & ~has_next_y, 0.0, 1.0).astype(F32)
    keep_x0 = jnp.where(has_prev_x, 1.0, 0.0).astype(F32)
    keep_x1 = jnp.where(has_next_x, 1.0, 0.0).astype(F32)

    def quarter_z(c, oz, row_is_chunk=False):
        lane = lax.broadcasted_iota(jnp.int32, (chunks if row_is_chunk else 1, 128), 1)
        if row_is_chunk:
            c = lax.broadcasted_iota(jnp.int32, (chunks, 128), 0)
        outside = ((oz == 0) & (c == 0) & (lane == 0)) | ((oz == 2) & (c == chunks - 1) & (lane == 127))
        return jnp.where(outside, 0.0, 0.25).astype(F32)

    def fold(read, keep_low, keep_high):
        before, behind = odd_parts(*(read(oy, TOP - 1) for oy in range(3)))
        ahead_0, ahead_1 = odd_parts(*(read(oy, TOP + 1) for oy in range(3)))
        own = [read(oy, TOP) for oy in range(3)]
        if keep_low is not None:
            own[0] = own[0] * keep_low
        e_minus, e_zero, e_plus = even_parts(*own)
        return before + e_minus, behind + e_zero + ahead_0, (e_plus + ahead_1) * keep_high

    def fold_fine(c, oz, ox, x):
        def read(oy, first):
            return fine[x, ox, oy, oz, pl.ds(c * fine_unit + first, half, stride=2), :]

        return fold(read, keep_first, keep_last)

    def fold_level(c, oz, ox, i_x):
        def read(oy, first):
            return level[i_x, ox, oy, oz, pl.ds(c * level_unit + first, quarter, stride=2), :]

        return fold(read, None, keep_last2)

    def over_z(body):
        def step(oz, carry):
            body(oz)
            return carry

        lax.fori_loop(0, 3, step, 0)

    def send_p(c):
        return pltpu.make_async_remote_copy(
            p_out.at[c], p_in.at[c], p_send.at[c], p_recv.at[c], device_id=(gx + 1, gy), device_id_type=MESH
        )

    def p_step(c):
        load_last_x(c).wait()

        def unit(oz):
            scale = quarter_z(c, oz)
            f = [fold_fine(c, oz, ox, 3) for ox in range(3)]
            for oy in range(3):
                a, b = odd_parts(f[0][oy], f[1][oy], f[2][oy])
                p_out[c, 0, oy, oz] = a * scale
                p_out[c, 1, oy, oz] = b * scale

        over_z(unit)

        @pl.when(c == 0)
        def _():
            waits = (
                has_next_x.astype(jnp.int32)
                + (has_prev_y & ~run_start).astype(jnp.int32)
                + (has_prev_y & ~run_start & has_prev_x & first_core).astype(jnp.int32)
                + (has_next_y & run_end).astype(jnp.int32)
                + (has_next_y & run_end & has_next_x & second_core).astype(jnp.int32)
            )

            @pl.when(waits > 0)
            def _():
                pl.semaphore_wait(barrier, waits)

                @pl.when(has_prev_y & ~run_start)
                def _():
                    pl.semaphore_signal(ready.at[0], inc=1, device_id=(gx, gy - 1), device_id_type=MESH)

                @pl.when(has_prev_y & ~run_start & has_prev_x & first_core)
                def _():
                    pl.semaphore_signal(ready.at[1], inc=1, device_id=(gx - 1, gy - 1), device_id_type=MESH)

        @pl.when(has_next_x)
        def _():
            send_p(c).start()

        @pl.when(c == 0)
        def _():
            for x in range(3):
                over(chunks, lambda c: load_edge(x, c).start())

    over(chunks, p_step)

    for x in (1, 2, 0):
        over(chunks, lambda c: load_body(x, c).start())

    for x in range(3):
        clear_fine(x)
    over(chunks, clear_level)

    def group(i, oz):
        return pl.ds((i * 3 + oz) * chunks, chunks)

    def fold_last(oz, ox, x):
        def read(oy, back):
            return fine[x, ox, oy, oz, pl.ds(fine_unit - back, chunks, stride=fine_unit), :]

        before, behind = odd_parts(*(read(oy, 3) for oy in range(3)))
        ahead = odd_parts(*(read(oy, 1) for oy in range(3)))
        e = even_parts(*(read(oy, 2) for oy in range(3)))
        return (before + e[0], behind + e[1] + ahead[0], e[2] + ahead[1]), ahead

    def edges(oz):
        scale = quarter_z(None, oz, True)
        f = [[fold_last(oz, ox, x) for ox in range(3)] for x in range(4)]

        def across(parts):
            a3, b3 = odd_parts(*parts[3])
            a1, b1 = odd_parts(*parts[1])
            e2 = even_parts(*parts[2])
            e0 = even_parts(parts[0][0] * keep_x0, parts[0][1], parts[0][2])
            first = [e0[0] * scale, (e0[1] + a1) * scale, (e0[2] + b1) * scale]
            second_x = [(a1 + e2[0]) * scale, (b1 + e2[1] + a3) * scale, (e2[2] + b3) * scale * keep_x1]
            return first, second_x, [a3 * scale, b3 * scale]

        onto = []
        for oy in range(2):
            first, second_x, beyond = across([[f[x][ox][1][oy] for ox in range(3)] for x in range(4)])
            onto.append(odd_parts(*second_x))
            for ox in range(3):
                y_out[group(ox * 2 + oy, oz), :] = first[ox]
                y_out[group(6 + ox * 2 + oy, oz), :] = second_x[ox]
            for ox in range(2):
                d_out[group(ox * 2 + oy, oz), :] = beyond[ox]
        own = [across([[f[x][ox][0][oy] for ox in range(3)] for x in range(4)]) for oy in range(3)]
        g = [[odd_parts(*(own[oy][i][ox] for oy in range(3))) for ox in range(3 if i < 2 else 2)] for i in range(3)]
        for oy in range(2):
            a, b = odd_parts(*(g[1][ox][oy] for ox in range(3)))
            e = even_parts(*(g[0][ox][oy] for ox in range(3)))
            y_out[group(12 + oy, oz), :] = e[0] * 0.25
            y_out[group(14 + oy, oz), :] = (e[1] + a) * 0.25
            y_out[group(16 + oy, oz), :] = (e[2] + b) * (0.25 * keep_x1)
            p_minus = g[2][0][oy]
            p_zero = g[2][0][oy] + (g[2][1][oy] + g[2][1][oy])
            onto_y = [onto[0][k] if oy == 0 else onto[0][k] + (onto[1][k] + onto[1][k]) for k in range(2)]
            d_out[group(4 + oy, oz), :] = (a + p_minus + onto_y[0]) * 0.25
            d_out[group(6 + oy, oz), :] = (b + p_zero + onto_y[1]) * 0.25

    for x in range(3):
        over(chunks, lambda c: load_edge(x, c).wait())
    over_z(edges)

    send_y = pltpu.make_async_remote_copy(
        y_out, y_in, edge_send.at[0], edge_recv.at[0], device_id=(gx, gy + 1), device_id_type=MESH
    )
    def copy_d(x, y, k):
        return pltpu.make_async_remote_copy(
            d_out, d_in, edge_send.at[k], edge_recv.at[k], device_id=(x, y), device_id_type=MESH
        )

    hand_d, send_d = copy_d(gx + 1, gy, 2), copy_d(gx + 1, gy + 1, 1)

    @pl.when(first_core & has_next_y & ~hand_late)
    def _():
        hand_d.start()

    @pl.when(second_core & run_end & has_next_x & has_next_y)
    def _():
        send_d.start()

    def add_corner(ref):
        for i in range(4):
            for k in (0, 1):
                to, at = pl.ds((i + 12 * k) * 3 * chunks, 3 * chunks), pl.ds((i + 4 * k) * 3 * chunks, 3 * chunks)
                ref[to, :] = ref[to, :] + d_in[at, :]

    def second_row(c):
        load_body(1, c).wait()
        load_body(2, c).wait()

        def unit(oz):
            scale = quarter_z(c, oz)
            f1 = [fold_fine(c, oz, ox, 1) for ox in range(3)]
            f2 = [fold_fine(c, oz, ox, 2) for ox in range(3)]
            for oy in range(3):
                a, b = odd_parts(f1[0][oy], f1[1][oy], f1[2][oy])
                e = even_parts(f2[0][oy], f2[1][oy], f2[2][oy])
                level[0, 1, oy, oz, inner(c), :] = a * scale
                level[0, 2, oy, oz, inner(c), :] = b * scale
                level[1, 0, oy, oz, inner(c), :] = (a + e[0]) * scale
                level[1, 1, oy, oz, inner(c), :] = (b + e[1]) * scale + p_out[c, 0, oy, oz]
                level[1, 2, oy, oz, inner(c), :] = (e[2] * scale + p_out[c, 1, oy, oz]) * keep_x1

        over_z(unit)

    over(chunks, second_row)

    def send_q(c):
        return pltpu.make_async_remote_copy(
            q_out.at[c], q_in.at[c], q_send.at[c], q_recv.at[c], device_id=(gx + 1, gy), device_id_type=MESH
        )

    detour_q = pltpu.make_async_remote_copy(
        q_out.at[0], q_relay, q_send.at[0], relay_sem.at[0], device_id=(gx + 1, gy + 1), device_id_type=MESH
    )
    relay_q = pltpu.make_async_remote_copy(
        q_relay, q_in.at[0], relay_sem.at[1], q_recv.at[0], device_id=(gx, gy - 1), device_id_type=MESH
    )

    def q_step(c):
        def unit(oz):
            f = [fold_level(c, oz, ox, 1) for ox in range(3)]
            for oy in range(3):
                a, b = odd_parts(f[0][oy], f[1][oy], f[2][oy])
                q_out[c, 0, oy, oz] = a * 0.25
                q_out[c, 1, oy, oz] = b * 0.25

        over_z(unit)

        @pl.when(has_next_x & ~(detour & (c == 0)))
        def _():
            send_q(c).start()

        @pl.when(detour & (c == 0))
        def _():
            pl.semaphore_wait(ready.at[1], 1)
            detour_q.start()

    over(chunks, q_step)

    def first_row(c):
        load_body(0, c).wait()

        def unit(oz):
            scale = quarter_z(c, oz)
            f = [fold_fine(c, oz, ox, 0) for ox in range(3)]
            for oy in range(3):
                e = even_parts(f[0][oy] * keep_x0, f[1][oy], f[2][oy])
                level[0, 0, oy, oz, inner(c), :] = e[0] * scale
                level[0, 1, oy, oz, inner(c), :] += e[1] * scale
                level[0, 2, oy, oz, inner(c), :] += e[2] * scale

        over_z(unit)

    over(chunks, first_row)

    for c in range(3):

        @pl.when(paced & (c < sent_first))
        def _():
            send_p(c).wait_send()

    @pl.when(second_core & has_next_y)
    def _():
        hand_d.wait_recv()
        add_corner(y_out)

    @pl.when(has_next_y & ~(giver & first_core & ~low_y))
    def _():
        @pl.when(~run_end)
        def _():
            pl.semaphore_wait(ready.at[0], 1)

        send_y.start()


    @pl.when(second_core & has_next_x & has_next_y & ~run_end)
    def _():
        @pl.when(~detour)
        def _():
            pl.semaphore_wait(ready.at[1], 1)

        send_d.start()

    @pl.when(relay)
    def _():
        detour_q.wait_recv()
        relay_q.start()

    def finish_one(c):
        @pl.when(has_prev_x)
        def _():
            send_p(c).wait_recv()

        def unit(oz):
            for oy in range(3):
                for ox in range(2):
                    level[0, ox, oy, oz, inner(c), :] += p_in[c, ox, oy, oz]
            f0 = [fold_level(c, oz, ox, 0) for ox in range(3)]
            f1 = [fold_level(c, oz, ox, 1) for ox in range(3)]
            for oy in range(3):
                e = even_parts(f0[0][oy], f0[1][oy], f0[2][oy])
                a, b = odd_parts(f1[0][oy], f1[1][oy], f1[2][oy])
                second[0, oy, oz, s_part(c), :] = e[0] * 0.25
                second[1, oy, oz, s_part(c), :] = (e[1] + a) * 0.25
                second[2, oy, oz, s_part(c), :] = (e[2] + b) * (0.25 * keep_x1)

        over_z(unit)

        @pl.when(giver & first_core & ~low_y & (c == arrived_first - 1))
        def _():
            send_y.start()

        @pl.when(hand_late & (c == arrived_first - 1))
        def _():
            hand_d.start()

    over(chunks, finish_one)

    def add_edges(oz):
        one_at, two_at = pl.ds(TOP, chunks, stride=level_unit), pl.ds(0, chunks, stride=quarter)
        e, o = [], []
        for oy in range(2):
            h = [[y_in[group(i_x * 6 + ox * 2 + oy, oz), :] for ox in range(3)] for i_x in range(2)]
            for i_x in range(2):
                for ox in range(3):
                    level[i_x, ox, oy, oz, one_at, :] = level[i_x, ox, oy, oz, one_at, :] + h[i_x][ox]
            e.append(even_parts(*h[0]))
            o.append(odd_parts(*h[1]))
        onto = [[e[oy][0], e[oy][1] + o[oy][0], (e[oy][2] + o[oy][1]) * keep_x1] for oy in range(2)]
        for ox in range(3):
            minus, centre = onto[0][ox], onto[0][ox] + (onto[1][ox] + onto[1][ox])
            for oy, value in ((0, minus), (1, centre)):
                value = value * 0.25 + y_in[group(12 + ox * 2 + oy, oz), :]
                second[ox, oy, oz, two_at, :] = second[ox, oy, oz, two_at, :] + value

    def finish_edges():
        send_y.wait_recv()

        @pl.when(first_core & has_prev_x)
        def _():
            send_d.wait_recv()
            add_corner(y_in)

        over_z(add_edges)

    taker = run_start & has_prev_y

    @pl.when(has_prev_y & ~run_start)
    def _():
        finish_edges()

    def finish_two(c):
        @pl.when(has_prev_x)
        def _():
            send_q(c).wait_recv()

        for oz in range(3):
            for ox in range(2):
                for oy in range(3):
                    second[ox, oy, oz, s_part(c), :] += q_in[c, ox, oy, oz]

    over(chunks, finish_two)

    @pl.when(taker)
    def _():
        finish_edges()

    @pl.when(has_next_x)
    def _():
        for c in range(chunks):
            send_q(c).wait_send()

    @pl.when(relay)
    def _():
        relay_q.wait_send()

    for c in range(chunks):

        @pl.when(has_next_x & ~(paced & (c < sent_first)))
        def _():
            send_p(c).wait_send()

    @pl.when(has_next_y)
    def _():
        send_y.wait_send()

    @pl.when(second_core & has_next_x & has_next_y)
    def _():
        send_d.wait_send()

    @pl.when(first_core & has_next_y)
    def _():
        hand_d.wait_send()


def write_kernel(level, second, one, two, sem):
    half, quarter, chunks = one.shape[4], two.shape[4], one.shape[5] // 128
    copies = []
    for c in range(chunks):
        lanes = pl.ds(c * 128, 128)
        for i_x in range(2):
            source = level.at[i_x, :, :, :, pl.ds(c * (TOP + half) + TOP, half), :]
            copies.append(pltpu.make_async_copy(source, one.at[:, :, :, i_x, :, lanes], sem.at[c, i_x]))
        source = second.at[:, :, :, pl.ds(c * quarter, quarter), :]
        copies.append(pltpu.make_async_copy(source, two.at[:, :, :, 0, :, lanes], sem.at[c, 2]))
    for i, copy in enumerate(copies):
        copy.start(priority=i % 2)
    for copy in copies:
        copy.wait()


def solution(mesh):
    n_x, n_y = mesh.shape["gx"], mesh.shape["gy"]
    z_run = n_y // 2

    def shard(stencil):
        _, _, _, cells_x, rows, nz = stencil.shape
        half, quarter, chunks = rows // 2, rows // 4, nz // 128
        vmem, hbm = pl.BlockSpec(memory_space=pltpu.VMEM), pl.BlockSpec(memory_space=pl.ANY)

        def kernel(*refs):
            transfer_kernel(n_x, n_y, z_run, *refs)

        level, second = pl.pallas_call(
            kernel,
            out_shape=(
                pltpu.VMEM((2, 3, 3, 3, chunks * (TOP + half), 128), F32),
                pltpu.VMEM((3, 3, 3, chunks * quarter, 128), F32),
            ),
            in_specs=[hbm],
            out_specs=(vmem, vmem),
            scratch_shapes=[
                pltpu.VMEM((cells_x, 3, 3, 3, chunks * (TOP + rows), 128), F32),
                pltpu.VMEM((chunks, 2, 3, 3, half, 128), F32),
                pltpu.VMEM((chunks, 2, 3, 3, half, 128), F32),
                pltpu.VMEM((chunks, 2, 3, 3, quarter, 128), F32),
                pltpu.VMEM((chunks, 2, 3, 3, quarter, 128), F32),
                pltpu.VMEM((54 * chunks, 128), F32),
                pltpu.VMEM((54 * chunks, 128), F32),
                pltpu.VMEM((24 * chunks, 128), F32),
                pltpu.VMEM((24 * chunks, 128), F32),
                pltpu.VMEM((2, 3, 3, quarter, 128), F32),
                pltpu.SemaphoreType.DMA((cells_x, chunks)),
                pltpu.SemaphoreType.DMA((cells_x - 1, chunks)),
                pltpu.SemaphoreType.DMA((chunks,)),
                pltpu.SemaphoreType.DMA((chunks,)),
                pltpu.SemaphoreType.DMA((chunks,)),
                pltpu.SemaphoreType.DMA((chunks,)),
                pltpu.SemaphoreType.DMA((3,)),
                pltpu.SemaphoreType.DMA((3,)),
                pltpu.SemaphoreType.DMA((2,)),
                pltpu.SemaphoreType.REGULAR((2,)),
            ],
            compiler_params=pltpu.CompilerParams(
                collective_id=0, has_side_effects=True, vmem_limit_bytes=56 * 2**20
            ),
        )(stencil)
        level, second = (pltpu.with_memory_space_constraint(v, pltpu.VMEM) for v in (level, second))
        return pl.pallas_call(
            write_kernel,
            out_shape=(
                jax.ShapeDtypeStruct((3, 3, 3, cells_x // 2, half, nz), F32),
                jax.ShapeDtypeStruct((3, 3, 3, cells_x // 4, quarter, nz), F32),
            ),
            in_specs=[vmem, vmem],
            out_specs=(hbm, hbm),
            scratch_shapes=[pltpu.SemaphoreType.DMA((chunks, 3))],
            compiler_params=pltpu.CompilerParams(vmem_limit_bytes=2**20),
        )(level, second)

    spec = P(None, None, None, "gx", "gy", None)
    return jax.shard_map(shard, mesh=mesh, in_specs=(spec,), out_specs=(spec, spec), check_vma=False)
```
